32 devices in a mesh: gx: 4 (over x, core), gy: 4 (over z), gz: 2 (over y).
Axes of the slice: x: 2, y: 2, z: 4, core: 2. Of those that a mesh axis runs over, the one named last changes fastest.
Arguments:
- initial_wind: float32 [3, 64, 512, 1024], P(None, 'gz', 'gx', 'gy'), may hold values from -4 to 4
- building_mask: int32 [64, 512, 1024], P('gz', 'gx', 'gy'), may hold values 0 or 1
- surface_flags: int32 [512, 1024], P('gx', 'gy'), may hold values from 0 to 3
- scalars: float32 [4, 64, 512, 1024], P(None, 'gz', 'gx', 'gy'), may hold values from 0 to 2
Outputs:
- corrected_wind: float32 [3, 64, 512, 1024], P(None, 'gz', 'gx', 'gy')
- transported: float32 [4, 64, 512, 1024], P(None, 'gz', 'gx', 'gy')
The draws below stay inside these ranges and needn't reach their ends.
Inputs may be any that keep to these rules, and one draw needn't show every extreme that they name: `building_mask`: 1 marks a building cell.
All inputs are finite; a program needn't handle non-finite values. No bound on the sum of `building_mask` on one device may be relied on, other than what follows from the above.
Results may differ from the reference program's by a relative error of at most 0.0003.
Values sent between devices are 32-bit elements; how exact they have to be, the bound alone decides.
No kernel may reach another device: no remote copies, remote signals or barrier semaphores. Data moves between devices by JAX's collectives and lax.ppermute only.
A program may use at most 512 MiB of HBM per device.

```python
import math
import jax
import jax.numpy as jnp
from jax import lax

NX = 512
NY = 1024
NZ = 64
SCALARS = 4


def with_ends(drawn, stream_key, smallest, top_value):
    longest = drawn.shape.index(max(drawn.shape))
    spots = []
    for shift in (0, 1):
        where = [jax.random.randint(jax.random.fold_in(stream_key, axis), (), 0, length) for axis, length in enumerate(drawn.shape)]
        where[longest] = (where[longest] + shift) % drawn.shape[longest]
        spots.append(tuple(where))
    return drawn.at[spots[0]].set(smallest).at[spots[1]].set(top_value)


def levels(rng, shape, shards, smallest, high):
    level = 1.0
    for axis_at, shards_of in shards:
        steps = jax.random.uniform(jax.random.fold_in(jax.random.fold_in(rng, 6), axis_at), (shards_of,), jnp.float32, smallest / len(shards), high / len(shards))
        level = level * jnp.repeat(jnp.exp(steps), shape[axis_at] // shards_of).reshape((-1,) + (1,) * (len(shape) - 1 - axis_at))
    return level


def centred(stream_key, shape, width, bound, cuts=(), kind=jnp.bfloat16):
    gain = levels(stream_key, shape, cuts, -0.22, 0.18) if cuts else 1.0
    array = jax.random.normal(stream_key, shape, jnp.float32) * width * gain
    return jnp.minimum(jnp.maximum(array, -bound), bound).astype(kind)


def setup_inputs(seed: int = 0) -> dict:
    seeds = jax.random.split(jax.random.key(seed), 5)
    return {
        "initial_wind": centred(seeds[0], (3, NZ, NX, NY), 1.0, 4.0, ((1, 2), (2, 4), (3, 4)), jnp.float32),
        "building_mask": with_ends((jax.random.randint(seeds[1], (NZ, NX, NY), 0, 5) < 1).astype(jnp.int32), jax.random.fold_in(seeds[1], 1), 0, 1),
        "surface_flags": with_ends(jax.random.randint(seeds[2], (NX, NY), 0, 4), jax.random.fold_in(seeds[2], 1), 0, 3).astype(jnp.int32),
        "scalars": jnp.clip(2.0 * jax.random.uniform(seeds[3], (SCALARS, NZ, NX, NY), jnp.float32) ** levels(seeds[3], (SCALARS, NZ, NX, NY), ((1, 2), (2, 4), (3, 4)), -0.2, 0.2), 0.0, 2.0),
    }


TIME_STEP = 0.2
ANISOTROPY = 4.0
DEPOSIT = ((0.0, 0.25, 0.75, 1.5), (0.0, 0.5, 1.0, 2.0), (0.1, 0.4, 0.8, 1.6), (0.0, 0.15, 1.25, 2.5))

def next_cell(values, direction):
    extent = values.shape[direction]
    zero_edge = jnp.zeros_like(lax.slice_in_dim(values, 0, 1, axis=direction))
    return jnp.concatenate([lax.slice_in_dim(values, 1, extent, axis=direction), zero_edge], axis=direction)

def prev_cell(values, direction):
    extent = values.shape[direction]
    zero_edge = jnp.zeros_like(lax.slice_in_dim(values, 0, 1, axis=direction))
    return jnp.concatenate([zero_edge, lax.slice_in_dim(values, 0, extent - 1, axis=direction)], axis=direction)

def basis_table(sine_kind, extent, spectral, spatial):
    wavenumber = spectral[:, None]
    position = spatial[None, :]
    if sine_kind:
        phase_index = (wavenumber + 1) * (2 * position + 1) % (4 * extent)
        weight = jnp.where(wavenumber == extent - 1, math.sqrt(1.0 / extent), math.sqrt(2.0 / extent))
        return (weight * jnp.sin(phase_index.astype(jnp.float32) * (math.pi / (2 * extent)))).astype(jnp.float32)
    phase_index = wavenumber * (2 * position + 1) % (4 * extent)
    weight = jnp.where(wavenumber == 0, math.sqrt(1.0 / extent), math.sqrt(2.0 / extent))
    return (weight * jnp.cos(phase_index.astype(jnp.float32) * (math.pi / (2 * extent)))).astype(jnp.float32)

def eigenvalues(sine_kind, extent, spectral):
    offset_one = 1 if sine_kind else 0
    half_angle = (spectral + offset_one).astype(jnp.float32) * (math.pi / (2 * extent))
    return 4.0 * jnp.sin(half_angle) ** 2

def denominator(index_z, index_x, index_y, total_z, total_x, total_y):
    return eigenvalues(True, total_x, index_x)[None, :, None] + eigenvalues(True, total_y, index_y)[None, None, :] + ANISOTROPY * eigenvalues(False, total_z, index_z)[:, None, None]

def contract(grid_field, matrix, direction):
    if direction == 0:
        return jnp.einsum('ka,abc->kbc', matrix, grid_field, precision=lax.Precision.HIGHEST)
    if direction == 1:
        return jnp.einsum('kb,abc->akc', matrix, grid_field, precision=lax.Precision.HIGHEST)
    return jnp.einsum('kc,abc->abk', matrix, grid_field, precision=lax.Precision.HIGHEST)

def limiter_ratio(demand, supply):
    binding = demand > supply
    return jnp.where(binding, supply / jnp.where(binding, demand, 1.0), 1.0)

def transport(concentration, wind_parts, spatial_axes, inside):
    anti_parts = []
    change = jnp.zeros_like(concentration)
    for component in range(3):
        direction = spatial_axes[component]
        velocity = wind_parts[component]
        downwind = next_cell(concentration, direction)
        upwind_flux = jnp.maximum(velocity, 0.0) * concentration + jnp.minimum(velocity, 0.0) * downwind
        central = 0.5 * velocity * (concentration + downwind)
        anti_parts.append(central - upwind_flux)
        change = change + (upwind_flux - prev_cell(upwind_flux, direction))
    trial_value = (concentration - TIME_STEP * change) * inside
    upper_bound = jnp.maximum(concentration, trial_value)
    lower_bound = jnp.minimum(concentration, trial_value)
    ceiling = upper_bound
    bottom = lower_bound
    for component in range(3):
        direction = spatial_axes[component]
        ceiling = jnp.maximum(ceiling, next_cell(upper_bound, direction))
        ceiling = jnp.maximum(ceiling, prev_cell(upper_bound, direction))
        bottom = jnp.minimum(bottom, next_cell(lower_bound, direction))
        bottom = jnp.minimum(bottom, prev_cell(lower_bound, direction))
    inflow = jnp.zeros_like(concentration)
    outflow = jnp.zeros_like(concentration)
    for component in range(3):
        direction = spatial_axes[component]
        anti_flux = anti_parts[component]
        before = prev_cell(anti_flux, direction)
        inflow = inflow + (jnp.maximum(before, 0.0) - jnp.minimum(anti_flux, 0.0))
        outflow = outflow + (jnp.maximum(anti_flux, 0.0) - jnp.minimum(before, 0.0))
    ratio_up = limiter_ratio(TIME_STEP * inflow, ceiling - trial_value) * inside
    ratio_down = limiter_ratio(TIME_STEP * outflow, trial_value - bottom) * inside
    correction = jnp.zeros_like(concentration)
    for component in range(3):
        direction = spatial_axes[component]
        anti_flux = anti_parts[component]
        limited = jnp.where(anti_flux >= 0.0, jnp.minimum(next_cell(ratio_up, direction), ratio_down), jnp.minimum(ratio_up, next_cell(ratio_down, direction))) * anti_flux
        correction = correction + (limited - prev_cell(limited, direction))
    return trial_value - TIME_STEP * correction

def ground_factor(surface_flags):
    deposit_rates = 1.0 - TIME_STEP * jnp.asarray(DEPOSIT, dtype=jnp.float32)
    factor = jnp.zeros((deposit_rates.shape[0],) + surface_flags.shape, jnp.float32)
    for surface in range(4):
        factor = factor + jnp.where(surface_flags[None] == surface, deposit_rates[:, surface][:, None, None], 0.0)
    return factor

def reference(initial_wind, building_mask, surface_flags, scalars):
    spatial_axes = (1, 2, 0)
    correction_gains = (0.5, 0.5, 0.5 * ANISOTROPY)
    openness = 1.0 - building_mask.astype(jnp.float32)
    face_open = []
    masked = []
    divergence = jnp.zeros(openness.shape, jnp.float32)
    for component in range(3):
        direction = spatial_axes[component]
        open_faces = openness * next_cell(openness, direction)
        masked_part = initial_wind[component] * open_faces
        face_open.append(open_faces)
        masked.append(masked_part)
        divergence = divergence + (masked_part - prev_cell(masked_part, direction))
    waves_z = jnp.arange(NZ, dtype=jnp.int32)
    waves_x = jnp.arange(NX, dtype=jnp.int32)
    waves_y = jnp.arange(NY, dtype=jnp.int32)
    cosine_z = basis_table(False, NZ, waves_z, waves_z)
    sine_x = basis_table(True, NX, waves_x, waves_x)
    sine_y = basis_table(True, NY, waves_y, waves_y)
    spectrum = contract(contract(contract(divergence, cosine_z, 0), sine_x, 1), sine_y, 2)
    solved = 2.0 * spectrum / denominator(waves_z, waves_x, waves_y, NZ, NX, NY)
    multiplier = contract(contract(contract(solved, sine_y.T, 2), sine_x.T, 1), cosine_z.T, 0)
    winds = []
    for component in range(3):
        direction = spatial_axes[component]
        gradient = next_cell(multiplier, direction) - multiplier
        winds.append((masked[component] + correction_gains[component] * gradient) * face_open[component])
    corrected_wind = jnp.stack(winds)
    factors = ground_factor(surface_flags)
    ground = (jnp.arange(NZ, dtype=jnp.int32) == 0)[:, None, None]

    def move_one(bundle):
        concentration, factor = bundle
        advected = transport(concentration, winds, spatial_axes, 1.0)
        return jnp.where(ground, advected * factor[None], advected)
    transported = lax.map(move_one, (scalars, factors))
    return (corrected_wind, transported)
```

```python
import functools
import math

import jax
import jax.numpy as jnp
import ml_dtypes
import numpy as np
from jax import lax
from jax.experimental import pallas as pl
from jax.experimental.pallas import tpu as pltpu
from jax.sharding import PartitionSpec as P

TIME_STEP = 0.2
ANISOTROPY = 4.0
GAINS = (0.5, 0.5, 0.5 * ANISOTROPY)
DEPOSIT = (
    (0.0, 0.25, 0.75, 1.5),
    (0.0, 0.5, 1.0, 2.0),
    (0.1, 0.4, 0.8, 1.6),
    (0.0, 0.15, 1.25, 2.5),
)
W = 3
RX = 8
LANES = 128
F32 = jnp.float32
BF16 = jnp.bfloat16
VMEM_LIMIT = 60 * 1024 * 1024


def params():
    return pltpu.CompilerParams(
        dimension_semantics=("arbitrary",), vmem_limit_bytes=VMEM_LIMIT
    )


def sine_half(extent):
    k = np.arange(extent)[:, None]
    n = np.arange(extent)[None, :]
    weight = np.where(k == extent - 1, math.sqrt(1.0 / extent), math.sqrt(2.0 / extent))
    return weight * np.sin(np.pi * ((k + 1) * (2 * n + 1) % (4 * extent)) / (2 * extent))


def cosine_half(extent):
    k = np.arange(extent)[:, None]
    n = np.arange(extent)[None, :]
    weight = np.where(k == 0, math.sqrt(1.0 / extent), math.sqrt(2.0 / extent))
    return weight * np.cos(np.pi * (k * (2 * n + 1) % (4 * extent)) / (2 * extent))


def sine_whole(extent):
    k = np.arange(extent)[:, None] + 1
    n = np.arange(extent)[None, :] + 1
    return math.sqrt(2.0 / (extent + 1)) * np.sin(np.pi * (k * n % (2 * extent + 2)) / (extent + 1))


def split_table(table):
    table = np.asarray(table, np.float32)
    high = table.astype(ml_dtypes.bfloat16)
    low = (table - high.astype(np.float32)).astype(ml_dtypes.bfloat16)
    return jnp.asarray(high), jnp.asarray(low)


def split_value(value):
    high = value.astype(BF16)
    return high, (value - high.astype(F32)).astype(BF16)


def mm(left, right):
    return jnp.dot(left, right, preferred_element_type=F32)


def table_left(high, low, value):
    v_high, v_low = split_value(value)
    return mm(high[...], v_high) + (mm(high[...], v_low) + mm(low[...], v_high))


def table_right(value, high, low):
    v_high, v_low = split_value(value)
    return mm(v_high, high[...]) + (mm(v_low, high[...]) + mm(v_high, low[...]))


def full(left, right):
    return jnp.dot(
        left, right, precision=lax.Precision.HIGHEST, preferred_element_type=F32
    )


def lines_kernel(x_ref, *refs):
    tables, o_ref = refs[:-1], refs[-1]
    count, _, rows, lanes = x_ref.shape
    value = x_ref[...].reshape(count * rows, lanes)
    if len(tables) == 2:
        result = table_left(*tables, value)
    else:
        result = full(tables[0][...], value)
    o_ref[...] = result.reshape(o_ref.shape)


def x_lines(blocks, tables, pieces):
    count, layers, rows, lanes = blocks.shape
    total = count * rows
    return pl.pallas_call(
        lines_kernel,
        grid=(layers,),
        in_specs=[
            pl.BlockSpec((count, 1, rows, lanes), lambda i: (0, i, 0, 0)),
        ]
        + [pl.BlockSpec((total, total), lambda i: (0, 0)) for _ in tables],
        out_specs=pl.BlockSpec((pieces, 1, total // pieces, lanes), lambda i: (0, i, 0, 0)),
        out_shape=jax.ShapeDtypeStruct((pieces, layers, total // pieces, lanes), F32),
        compiler_params=params(),
    )(blocks, *tables)


def forward_kernel(x_ref, s_high, s_low, k_high, k_low, lam_ref, ey_ref, ends_ref, b_ref, fl_ref):
    total_z, rows, lanes = x_ref.shape
    value = x_ref[...].reshape(total_z * rows, lanes)
    spectrum = table_left(k_high, k_low, table_right(value, s_high, s_low))
    b_ref[...] = spectrum.reshape(b_ref.shape)
    local = spectrum / (lam_ref[0] + ey_ref[...])
    fl_ref[0] = lax.dot_general(
        ends_ref[...],
        local,
        (((1,), (1,)), ((), ())),
        precision=lax.Precision.HIGHEST,
        preferred_element_type=F32,
    )


def backward_kernel(b_ref, ab_ref, s_ref, k_ref, lam_ref, ey_ref, ends_ref, u_ref):
    total_z, rows, lanes = b_ref.shape
    spectrum = b_ref[...].reshape(total_z * rows, lanes)
    ends = lax.dot_general(
        ab_ref[0],
        ends_ref[...],
        (((0,), (0,)), ((), ())),
        precision=lax.Precision.HIGHEST,
        preferred_element_type=F32,
    )
    solved = (spectrum + ends) / (lam_ref[0] + ey_ref[...])
    u_ref[...] = full(k_ref[...], full(solved, s_ref[...])).reshape(u_ref.shape)


def solve(source, scalars, scalar_z):
    local_z, local_x, local_y = source.shape
    nx, ny, nz = lax.axis_size("gx"), lax.axis_size("gy"), lax.axis_size("gz")
    total_x, total_z = local_x * nx, local_z * nz
    group = nx * nz
    layers = local_z // nx
    part_x = total_x // group
    tiles = part_x // 8
    pair_rows = total_z * 8
    chunk = lax.axis_index("gz") * nx + lax.axis_index("gx")

    e_x = 4.0 * np.sin(np.pi * (np.arange(total_x) + 1) / (2 * total_x)) ** 2
    e_z = 4.0 * np.sin(np.pi * np.arange(total_z) / (2 * total_z)) ** 2
    lam = ANISOTROPY * e_z[:, None] + e_x[None, :]
    lam = lam.reshape(total_z, group, tiles, 8).transpose(1, 2, 0, 3).reshape(group, tiles, pair_rows)
    theta = np.log1p(lam / 2 + np.sqrt(lam + lam * lam / 4))
    whole = np.expm1(-2 * (local_y + 1) * theta)
    alpha = np.exp(-theta) * np.expm1(-2 * local_y * theta) / whole
    beta = np.exp(-local_y * theta) * np.expm1(-2 * theta) / whole
    response = [alpha - beta * beta / (1 + alpha)]
    inverse = [1 / (1 + alpha)]
    for _ in range(1, ny):
        inverse.append(1 / (1 - alpha * response[-1]))
        response.append(alpha + beta * beta * response[-1] * inverse[-1])
    closing = 1 / (1 + response[-1])

    def mine(table):
        return lax.dynamic_index_in_dim(jnp.asarray(table, F32), chunk, 0, keepdims=False)

    basis = sine_whole(local_y)
    e_y = 4.0 * np.sin(np.pi * (np.arange(local_y) + 1) / (2 * (local_y + 1))) ** 2
    ends = np.zeros((8, local_y))
    ends[0], ends[1] = basis[:, 0], basis[:, -1]
    ends = jnp.asarray(ends, F32)
    ey = jnp.asarray(e_y[None, :], F32)
    lam_rows = mine(lam)[:, :, None]
    s_high, s_low = split_table(basis)
    cosine = np.kron(cosine_half(total_z), np.eye(8))
    forward_z = split_table(2.0 * cosine)
    backward_z = jnp.asarray(cosine.T, F32)

    together = lax.optimization_barrier
    source, scalar_z = together((source, scalar_z))
    blocks = source.reshape(nx, layers, local_x, local_y)
    scalar_x = x_halo((scalars,), *scalar_z)
    blocks = lax.all_to_all(blocks, "gx", 0, 0)
    blocks, scalar_x = together((blocks, scalar_x))
    sine_x = sine_half(total_x)
    blocks = x_lines(blocks, split_table(sine_x), group)
    scalar_pack = y_pack((scalars,), *scalar_z, *scalar_x)
    blocks = lax.all_to_all(blocks, ("gz", "gx"), 0, 0)
    blocks, scalar_pack = together((blocks, scalar_pack))
    scalar_y = shift_pair(*scalar_pack, "gy")
    columns = blocks.reshape(total_z, part_x, local_y)

    cube = pl.BlockSpec((total_z, 8, local_y), lambda i: (0, i, 0))
    small = pl.BlockSpec((1, 8, pair_rows), lambda i: (i, 0, 0))
    tables = [
        pl.BlockSpec((local_y, local_y), lambda i: (0, 0)),
        pl.BlockSpec((local_y, local_y), lambda i: (0, 0)),
        pl.BlockSpec((pair_rows, pair_rows), lambda i: (0, 0)),
        pl.BlockSpec((pair_rows, pair_rows), lambda i: (0, 0)),
        pl.BlockSpec((1, pair_rows, 1), lambda i: (i, 0, 0)),
        pl.BlockSpec((1, local_y), lambda i: (0, 0)),
        pl.BlockSpec((8, local_y), lambda i: (0, 0)),
    ]
    spectrum, edge = pl.pallas_call(
        forward_kernel,
        grid=(tiles,),
        in_specs=[cube] + tables,
        out_specs=[cube, small],
        out_shape=[
            jax.ShapeDtypeStruct(columns.shape, F32),
            jax.ShapeDtypeStruct((tiles, 8, pair_rows), F32),
        ],
        compiler_params=params(),
    )(columns, s_high, s_low, *forward_z, lam_rows, ey, ends)

    every = lax.all_gather(edge[:, :2], "gy")
    al, be = mine(alpha), mine(beta)
    re = [mine(r) for r in response]
    inv = [mine(r) for r in inverse]
    first_in = [every[p, :, 0] for p in range(ny)]
    last_in = [every[p, :, 1] for p in range(ny)]
    carried = [last_in[0] - be * first_in[0] * inv[0]]
    for p in range(1, ny):
        prior = carried[-1]
        carried.append(
            last_in[p] + be * (prior + re[p - 1] * (first_in[p] + al * prior) * inv[p])
        )
    first, last = [None] * ny, [None] * ny
    last[ny - 1] = carried[ny - 1] * mine(closing)
    above = -last[ny - 1]
    for p in range(ny - 1, -1, -1):
        if p < ny - 1:
            last[p] = carried[p] + re[p] * above
        if p > 0:
            first[p] = (first_in[p] + al * carried[p - 1] + be * above) * inv[p]
        else:
            first[p] = (first_in[p] + be * above) * inv[p]
        above = first[p]
    below = jnp.stack([-first[0]] + last[:-1])
    above = jnp.stack(first[1:] + [-last[-1]])
    place = lax.axis_index("gy")
    below = lax.dynamic_index_in_dim(below, place, 0, keepdims=False)
    above = lax.dynamic_index_in_dim(above, place, 0, keepdims=False)
    sides = jnp.stack([below, above] + [jnp.zeros_like(below)] * 6, 1)

    columns = pl.pallas_call(
        backward_kernel,
        grid=(tiles,),
        in_specs=[cube, small, tables[0], tables[2]] + tables[4:],
        out_specs=cube,
        out_shape=jax.ShapeDtypeStruct(columns.shape, F32),
        compiler_params=params(),
    )(spectrum, sides, jnp.asarray(basis, F32), backward_z, lam_rows, ey, ends)

    blocks = columns.reshape(group, layers, part_x, local_y)
    blocks = lax.all_to_all(blocks, ("gz", "gx"), 0, 0)
    blocks, scalar_y = together((blocks, scalar_y))
    blocks = x_lines(blocks, (jnp.asarray(sine_x.T, F32),), nx)
    blocks = lax.all_to_all(blocks, "gx", 0, 0)
    return blocks.reshape(local_z, local_x, local_y), scalar_z + scalar_x + scalar_y


def shift_pair(low_part, high_part, axis):
    count = lax.axis_size(axis)
    up = [(i, i + 1) for i in range(count - 1)]
    down = [(target, source) for source, target in up]
    return lax.ppermute(high_part, axis, up), lax.ppermute(low_part, axis, down)


def pack_kernel(groups, span, *refs):
    count = len(groups)
    firsts, finals = refs[:count], refs[count : 2 * count]
    zlf, zll, zhf, zhl, xlf, xll, xhf, xhl, lo_ref, hi_ref = refs[2 * count :]
    step = pl.program_id(0)
    depth = pl.num_programs(0) * span
    rows = firsts[0].shape[2]
    lane = lax.broadcasted_iota(jnp.int32, (1, LANES), 1)

    def packed(k, first, final, old):
        keep = (lane >= W * k) & (lane < W * k + W)
        low = jnp.where(keep, pltpu.roll(first, lax.rem(W * k, LANES), 1), old[0])
        high = jnp.where(keep, pltpu.roll(final, lax.rem(W * k + W, LANES), 1), old[1])
        return low, high

    inner = slice(RX, RX + rows)

    @pl.when(step == 0)
    def _():
        for field in range(sum(groups)):
            for begin, first, final in ((0, xlf, xll), (RX + rows, xhf, xhl)):
                old = (jnp.zeros((RX, LANES), F32),) * 2
                for k in range(first.shape[1]):
                    old = packed(jnp.int32(k), first[field, k], final[field, k], old)
                lo_ref[field, begin : begin + RX, :] = old[0]
                hi_ref[field, begin : begin + RX, :] = old[1]
            old = (jnp.zeros((rows, LANES), F32),) * 2
            for k in range(W):
                old = packed(jnp.int32(k), zlf[field, k], zll[field, k], old)
                old = packed(W + depth + k, zhf[field, k], zhl[field, k], old)
            lo_ref[field, inner, :] = old[0]
            hi_ref[field, inner, :] = old[1]

    field = 0
    for at, size in enumerate(groups):
        for index in range(size):
            old = (lo_ref[field, inner, :], hi_ref[field, inner, :])
            for j in range(span):
                old = packed(
                    W + step * span + j, firsts[at][index, j], finals[at][index, j], old
                )
            lo_ref[field, inner, :] = old[0]
            hi_ref[field, inner, :] = old[1]
            field += 1


def joined(arrays, pick):
    parts = [pick(a) for a in arrays]
    return parts[0] if len(parts) == 1 else jnp.concatenate(parts, 0)


def z_halo(arrays, after=None):
    local_z = arrays[0].shape[1]
    first = joined(arrays, lambda a: a[:, :W])
    final = joined(arrays, lambda a: a[:, local_z - W :])
    if after is not None:
        first, final, _ = lax.optimization_barrier((first, final, after))
    return shift_pair(first, final, "gz")


def x_halo(arrays, z_low, z_high):
    local_x = arrays[0].shape[2]

    def rows(begin):
        cut = lambda a: a[:, :, begin : begin + RX]
        return jnp.concatenate([cut(z_low), joined(arrays, cut), cut(z_high)], 1)

    return shift_pair(rows(0), rows(local_x - RX), "gx")


def y_pack(arrays, z_low, z_high, x_low, x_high):
    local_z, local_x, local_y = arrays[0].shape[1:]
    groups = tuple(a.shape[0] for a in arrays)
    fields = sum(groups)
    final = local_y // LANES - 1
    span = 8

    def edge(shape, at):
        return pl.BlockSpec(shape[:3] + (LANES,), lambda k: (0, 0, 0, at))

    def part(size, at):
        return pl.BlockSpec((size, span, local_x, LANES), lambda k: (0, k, 0, at))

    specs = [part(g, 0) for g in groups] + [part(g, final) for g in groups]
    operands = list(arrays) * 2
    for array in (z_low, z_high, x_low, x_high):
        specs += [edge(array.shape, 0), edge(array.shape, final)]
        operands += [array, array]
    shape = (fields, local_x + 2 * RX, LANES)
    return pl.pallas_call(
        functools.partial(pack_kernel, groups, span),
        grid=(local_z // span,),
        in_specs=specs,
        out_specs=[pl.BlockSpec(shape, lambda k: (0, 0, 0))] * 2,
        out_shape=[jax.ShapeDtypeStruct(shape, F32)] * 2,
        compiler_params=params(),
    )(*operands)


def halos(arrays):
    z_part = z_halo(arrays)
    x_part = x_halo(arrays, *z_part)
    return z_part + x_part + shift_pair(*y_pack(arrays, *z_part, *x_part), "gy")


def halo_specs(fields, local_z, local_x, local_y, plane_of):
    return [
        pl.BlockSpec(
            (fields, 1, local_x, local_y), lambda k: (0, jnp.minimum(plane_of(k), W - 1), 0, 0)
        ),
        pl.BlockSpec(
            (fields, 1, local_x, local_y),
            lambda k: (0, jnp.maximum(plane_of(k) - W - local_z, 0), 0, 0),
        ),
        pl.BlockSpec((fields, 1, RX, local_y), lambda k: (0, plane_of(k), 0, 0)),
        pl.BlockSpec((fields, 1, RX, local_y), lambda k: (0, plane_of(k), 0, 0)),
        pl.BlockSpec((fields, local_x + 2 * RX, LANES), lambda k: (0, 0, 0)),
        pl.BlockSpec((fields, local_x + 2 * RX, LANES), lambda k: (0, 0, 0)),
    ]


def assemble(k, local_z, mains, halo, put):
    z_low, z_high, x_low, x_high, y_low, y_high = halo
    local_x, local_y = z_low.shape[2:]
    every = slice(0, local_x + 2 * RX)
    inner = slice(RX, RX + local_x)
    wide = slice(0, local_y)
    lane = lax.broadcasted_iota(jnp.int32, (1, LANES), 1)
    up = lax.rem(2 * LANES - W * k, LANES)
    down = lax.rem(2 * LANES - W * k - W, LANES)
    field = 0
    for main in mains:
        for index in range(main.shape[0]):

            @pl.when((k >= W) & (k < W + local_z))
            def _():
                put(field, inner, wide, main[index, 0])

            @pl.when(k < W)
            def _():
                put(field, inner, wide, z_low[field, 0])

            @pl.when(k >= W + local_z)
            def _():
                put(field, inner, wide, z_high[field, 0])

            put(field, slice(0, RX), wide, x_low[field, 0])
            put(field, slice(RX + local_x, 2 * RX + local_x), wide, x_high[field, 0])
            put(
                field,
                every,
                slice(local_y, local_y + LANES),
                jnp.where(
                    lane < LANES // 2,
                    pltpu.roll(y_high[field], up, 1),
                    pltpu.roll(y_low[field], down, 1),
                ),
            )
            field += 1


def next_y(value):
    return pltpu.roll(value, value.shape[1] - 1, 1)


def prev_y(value):
    return pltpu.roll(value, 1, 1)


def next_x(value, after):
    row = lax.broadcasted_iota(jnp.int32, value.shape, 0)
    return pltpu.roll(jnp.where(row == 0, after, value), 7, 0)


def prev_x(value, before):
    row = lax.broadcasted_iota(jnp.int32, value.shape, 0)
    return pltpu.roll(jnp.where(row == 7, before, value), 1, 0)


def divergence_kernel(local_z, wind, opened, *refs):
    halo, out, cell, face_z = refs[:6], refs[6], refs[7], refs[8]
    k = pl.program_id(0) + W - 1
    local_x, local_y = out.shape[1:]
    lanes = local_y + LANES
    now, old = lax.rem(k, 2), lax.rem(k + 1, 2)

    def put(field, rows, wide, value):
        cell[now, field, rows, wide] = value

    assemble(k, local_z, (wind, opened), halo, put)
    count = local_x // 8 + 2
    before = jnp.zeros((8, lanes), F32)
    for i in range(count - 1):
        here, after = slice(8 * i, 8 * i + 8), slice(8 * i + 8, 8 * i + 16)
        open_cells = cell[old, 3, here, :]
        flux_x = cell[old, 0, here, :] * (open_cells * next_x(open_cells, cell[old, 3, after, :]))
        flux_y = cell[old, 1, here, :] * (open_cells * next_y(open_cells))
        flux_z = cell[old, 2, here, :] * (open_cells * cell[now, 3, here, :])
        if i > 0:
            total = (flux_x - prev_x(flux_x, before)) + (flux_y - prev_y(flux_y))
            total = total + (flux_z - face_z[here, :])
            out[0, 8 * i - 8 : 8 * i, :] = total[:, :local_y]
        face_z[here, :] = flux_z
        before = flux_x


def divergence(wind, opened, wind_halo):
    local_z, local_x, local_y = wind.shape[1:]
    plane_of = lambda k: k + W - 1
    middle = lambda k: (0, jnp.clip(plane_of(k) - W, 0, local_z - 1), 0, 0)
    lanes = local_y + LANES
    rows = local_x + 2 * RX
    return pl.pallas_call(
        functools.partial(divergence_kernel, local_z),
        grid=(local_z + 2,),
        in_specs=[
            pl.BlockSpec((3, 1, local_x, local_y), middle),
            pl.BlockSpec((1, 1, local_x, local_y), middle),
        ]
        + halo_specs(4, local_z, local_x, local_y, plane_of),
        out_specs=pl.BlockSpec(
            (1, local_x, local_y), lambda k: (jnp.clip(k - 2, 0, local_z - 1), 0, 0)
        ),
        out_shape=jax.ShapeDtypeStruct((local_z, local_x, local_y), F32),
        scratch_shapes=[pltpu.VMEM((2, 4, rows, lanes), F32), pltpu.VMEM((rows, lanes), F32)],
        compiler_params=params(),
    )(wind, opened, *wind_halo)


def limiter(demand, supply):
    binding = demand > supply
    return jnp.where(binding, supply / jnp.where(binding, demand, 1.0), 1.0)


def transport_kernel(local_z, scalar_count, *refs):
    scal, sc_halo = refs[0], refs[1:7]
    wind, opened, wi_halo = refs[7], refs[8], refs[9:15]
    mult, mu_halo = refs[15], refs[16:22]
    factor, wind_out, out = refs[22:25]
    speed, cell, kept = refs[25], refs[26], refs[27:]
    conc, trial, upper, lower, anti, ratio, low_z, lim_z, edge, result = (
        kept[at * scalar_count : (at + 1) * scalar_count] for at in range(10)
    )
    k = pl.program_id(0)
    local_x, local_y = out.shape[2:]
    lanes = local_y + LANES
    count = local_x // 8 + 2
    s0, s1, s2, s3 = (lax.rem(k + 4 - d, 4) for d in range(4))
    now, old = lax.rem(k, 2), lax.rem(k + 1, 2)

    def put_scalar(field, rows, wide, value):
        conc[field][s0, rows, wide] = value

    def put_wind(field, rows, wide, value):
        cell[now, field, rows, wide] = value

    def put_mult(field, rows, wide, value):
        cell[now, 4, rows, wide] = value

    assemble(k, local_z, (scal,), sc_halo, put_scalar)
    assemble(k, local_z, (wind, opened), wi_halo, put_wind)
    assemble(k, local_z, (mult,), mu_halo, put_mult)

    def chunk(i):
        return pl.ds(pl.multiple_of(i * 8, 8), 8)

    def column(i, _):
        here = chunk(i)
        after = chunk(jnp.minimum(i + 1, count - 1))
        before = chunk(jnp.maximum(i - 1, 0))

        cells, multiplier = cell[old, 3, here, :], cell[old, 4, here, :]
        neighbours = (
            (next_x(cells, cell[old, 3, after, :]), next_x(multiplier, cell[old, 4, after, :])),
            (next_y(cells), next_y(multiplier)),
            (cell[now, 3, here, :], cell[now, 4, here, :]),
        )
        speeds, halves, sizes = [], [], []
        for d in range(3):
            open_next, mult_next = neighbours[d]
            face = cells * open_next
            value = (cell[old, d, here, :] * face + GAINS[d] * (mult_next - multiplier)) * face
            speeds.append(value)
            halves.append((0.5 * TIME_STEP) * value)
            sizes.append(jnp.abs(halves[-1]))
        for d in range(3):
            speed[d, here, :] = speeds[d][:, :local_y]

        for s in range(scalar_count):
            c = conc[s][s1, here, :]
            downwind = (next_x(c, conc[s][s1, after, :]), next_y(c), conc[s][s0, here, :])
            antis, lows = [], []
            for d in range(3):
                a = sizes[d] * (downwind[d] - c)
                antis.append(a)
                lows.append(halves[d] * (downwind[d] + c) - a)
            change = (lows[0] - prev_x(lows[0], edge[s][0])) + (lows[1] - prev_y(lows[1]))
            t_new = c - (change + (lows[2] - low_z[s][here, :]))
            u_new, l_new = jnp.maximum(c, t_new), jnp.minimum(c, t_new)

            u, l = upper[s][s2, here, :], lower[s][s2, here, :]
            ceiling = jnp.maximum(
                jnp.maximum(u, u_new),
                jnp.maximum(
                    next_x(u, upper[s][s2, after, :]), prev_x(u, upper[s][s2, before, :])
                ),
            )
            ceiling = jnp.maximum(
                jnp.maximum(ceiling, upper[s][s3, here, :]), jnp.maximum(next_y(u), prev_y(u))
            )
            bottom = jnp.minimum(
                jnp.minimum(l, l_new),
                jnp.minimum(
                    next_x(l, lower[s][s2, after, :]), prev_x(l, lower[s][s2, before, :])
                ),
            )
            bottom = jnp.minimum(
                jnp.minimum(bottom, lower[s][s3, here, :]), jnp.minimum(next_y(l), prev_y(l))
            )
            a_x, a_y, a_z = (anti[s][s2, d, here, :] for d in range(3))
            befores = (
                prev_x(a_x, anti[s][s2, 0, before, :]),
                prev_y(a_y),
                anti[s][s3, 2, here, :],
            )
            inflow, outflow = 0.0, 0.0
            for a, b in zip((a_x, a_y, a_z), befores):
                inflow = inflow + (jnp.maximum(b, 0.0) - jnp.minimum(a, 0.0))
                outflow = outflow + (jnp.maximum(a, 0.0) - jnp.minimum(b, 0.0))
            t_mid = trial[s][s2, here, :]
            up_new = limiter(inflow, ceiling - t_mid)
            down_new = limiter(outflow, t_mid - bottom)

            r_up, r_down = ratio[s][old, 0, here, :], ratio[s][old, 1, here, :]
            nexts = (
                (
                    next_x(r_up, ratio[s][old, 0, after, :]),
                    next_x(r_down, ratio[s][old, 1, after, :]),
                ),
                (next_y(r_up), next_y(r_down)),
                (up_new, down_new),
            )
            limited = []
            for d in range(3):
                a = anti[s][s3, d, here, :]
                share = jnp.where(
                    a >= 0.0, jnp.minimum(nexts[d][0], r_down), jnp.minimum(r_up, nexts[d][1])
                )
                limited.append(share * a)
            moved = limited[0] - prev_x(limited[0], edge[s][1])
            moved = moved + (limited[1] - prev_y(limited[1])) + (limited[2] - lim_z[s][here, :])
            final = trial[s][s3, here, :] - moved

            result[s][here, :] = final[:, :local_y]
            lim_z[s][here, :] = limited[2]
            edge[s][1] = limited[0]
            ratio[s][now, 0, here, :] = up_new
            ratio[s][now, 1, here, :] = down_new
            trial[s][s1, here, :] = t_new
            upper[s][s1, here, :] = u_new
            lower[s][s1, here, :] = l_new
            low_z[s][here, :] = lows[2]
            edge[s][0] = lows[0]
            for d in range(3):
                anti[s][s1, d, here, :] = antis[d]
        return 0

    lax.fori_loop(0, count, column, 0)
    inner = slice(RX, RX + local_x)

    @pl.when((k > W) & (k <= W + local_z))
    def _():
        for d in range(3):
            wind_out[d, 0] = speed[d, inner, :]

    @pl.when(k > 2 * W)
    def _():
        for s in range(scalar_count):
            out[s, 0] = result[s][inner, :]

    @pl.when(k == 2 * W)
    def _():
        for s in range(scalar_count):
            out[s, 0] = result[s][inner, :] * factor[s]


def transport(scalars, sc_halo, wind, opened, wi_halo, mult, mu_halo, factor):
    n, local_z, local_x, local_y = scalars.shape
    same = lambda k: k
    middle = lambda k: (0, jnp.clip(k - W, 0, local_z - 1), 0, 0)
    lanes = local_y + LANES
    rows = local_x + 2 * RX
    plane = (rows, lanes)

    def main(count):
        return [pl.BlockSpec((count, 1, local_x, local_y), middle)]

    def halo(count):
        return halo_specs(count, local_z, local_x, local_y, same)

    return pl.pallas_call(
        functools.partial(transport_kernel, local_z, n),
        grid=(local_z + 2 * W,),
        in_specs=main(n)
        + halo(n)
        + main(3)
        + main(1)
        + halo(4)
        + main(1)
        + halo(1)
        + [pl.BlockSpec((n, local_x, local_y), lambda k: (0, 0, 0))],
        out_specs=[
            pl.BlockSpec(
                (3, 1, local_x, local_y), lambda k: (0, jnp.clip(k - 1 - W, 0, local_z - 1), 0, 0)
            ),
            pl.BlockSpec(
                (n, 1, local_x, local_y), lambda k: (0, jnp.clip(k - 2 * W, 0, local_z - 1), 0, 0)
            ),
        ],
        out_shape=[
            jax.ShapeDtypeStruct((3, local_z, local_x, local_y), F32),
            jax.ShapeDtypeStruct(scalars.shape, F32),
        ],
        scratch_shapes=[pltpu.VMEM((3, rows, local_y), F32), pltpu.VMEM((2, 5) + plane, F32)]
        + [
            pltpu.VMEM(shape, F32)
            for shape in (
                (4,) + plane,
                (4,) + plane,
                (4,) + plane,
                (4,) + plane,
                (4, 3) + plane,
                (2, 2) + plane,
                plane,
                plane,
                (2, 8, lanes),
                (rows, local_y),
            )
            for _ in range(n)
        ],
        compiler_params=params(),
    )(scalars, *sc_halo, wind, opened, *wi_halo, mult, *mu_halo, factor)


def ground_factor(surface_flags):
    rates = 1.0 - TIME_STEP * np.asarray(DEPOSIT, np.float32)
    factor = jnp.zeros((len(DEPOSIT),) + surface_flags.shape, F32)
    for surface in range(4):
        column = jnp.asarray(rates[:, surface], F32)[:, None, None]
        factor = factor + jnp.where(surface_flags[None] == surface, column, 0.0)
    return jnp.where(lax.axis_index("gz") == 0, factor, 1.0)


def body(initial_wind, building_mask, surface_flags, scalars):
    opened = (1.0 - building_mask.astype(F32))[None]
    wind_z = z_halo((initial_wind, opened))
    scalar_z = z_halo((scalars,), wind_z)
    wind_x = x_halo((initial_wind, opened), *wind_z)
    wind_y = shift_pair(*y_pack((initial_wind, opened), *wind_z, *wind_x), "gy")
    wind_halo = wind_z + wind_x + wind_y
    source = divergence(initial_wind, opened, wind_halo)
    multiplier, scalar_halo = solve(source, scalars, scalar_z)
    multiplier = multiplier[None]
    mult_halo = halos((multiplier,))
    corrected, transported = transport(
        scalars,
        scalar_halo,
        initial_wind,
        opened,
        wind_halo,
        multiplier,
        mult_halo,
        ground_factor(surface_flags),
    )
    return (corrected, transported)


def solution(mesh):
    in_specs = (
        P(None, "gz", "gx", "gy"),
        P("gz", "gx", "gy"),
        P("gx", "gy"),
        P(None, "gz", "gx", "gy"),
    )
    out_specs = (P(None, "gz", "gx", "gy"), P(None, "gz", "gx", "gy"))
    return jax.shard_map(body, mesh=mesh, in_specs=in_specs, out_specs=out_specs, check_vma=False)
```

```python
import functools
import math

import jax
import jax.numpy as jnp
import ml_dtypes
import numpy as np
from jax import lax
from jax.experimental import pallas as pl
from jax.experimental.pallas import tpu as pltpu
from jax.sharding import PartitionSpec as P

TIME_STEP = 0.2
ANISOTROPY = 4.0
GAINS = (0.5, 0.5, 0.5 * ANISOTROPY)
DEPOSIT = (
    (0.0, 0.25, 0.75, 1.5),
    (0.0, 0.5, 1.0, 2.0),
    (0.1, 0.4, 0.8, 1.6),
    (0.0, 0.15, 1.25, 2.5),
)
W = 3
RX = 8
LEAD = 16
LANES = 128
F32 = jnp.float32
BF16 = jnp.bfloat16
VMEM_LIMIT = 60 * 1024 * 1024


def params():
    return pltpu.CompilerParams(
        dimension_semantics=("arbitrary",), vmem_limit_bytes=VMEM_LIMIT
    )


def sine_half(extent):
    k = np.arange(extent)[:, None]
    n = np.arange(extent)[None, :]
    weight = np.where(k == extent - 1, math.sqrt(1.0 / extent), math.sqrt(2.0 / extent))
    return weight * np.sin(np.pi * ((k + 1) * (2 * n + 1) % (4 * extent)) / (2 * extent))


def cosine_half(extent):
    k = np.arange(extent)[:, None]
    n = np.arange(extent)[None, :]
    weight = np.where(k == 0, math.sqrt(1.0 / extent), math.sqrt(2.0 / extent))
    return weight * np.cos(np.pi * (k * (2 * n + 1) % (4 * extent)) / (2 * extent))


def sine_whole(extent):
    k = np.arange(extent)[:, None] + 1
    n = np.arange(extent)[None, :] + 1
    return math.sqrt(2.0 / (extent + 1)) * np.sin(np.pi * (k * n % (2 * extent + 2)) / (extent + 1))


def split_table(table):
    table = np.asarray(table, np.float32)
    high = table.astype(ml_dtypes.bfloat16)
    low = (table - high.astype(np.float32)).astype(ml_dtypes.bfloat16)
    return jnp.asarray(high), jnp.asarray(low)


def split_value(value):
    high = value.astype(BF16)
    return high, (value - high.astype(F32)).astype(BF16)


def mm(left, right):
    return jnp.dot(left, right, preferred_element_type=F32)


def table_left(high, low, value):
    v_high, v_low = split_value(value)
    return mm(high[...], v_high) + (mm(high[...], v_low) + mm(low[...], v_high))


def table_right(value, high, low):
    v_high, v_low = split_value(value)
    return mm(v_high, high[...]) + (mm(v_low, high[...]) + mm(v_high, low[...]))


def full(left, right):
    return jnp.dot(
        left, right, precision=lax.Precision.HIGHEST, preferred_element_type=F32
    )


def lines_kernel(x_ref, *refs):
    tables, o_ref = refs[:-1], refs[-1]
    count, _, rows, lanes = x_ref.shape
    value = x_ref[...].reshape(count * rows, lanes)
    if len(tables) == 2:
        result = table_left(*tables, value)
    else:
        result = full(tables[0][...], value)
    o_ref[...] = result.reshape(o_ref.shape)


def x_lines(blocks, tables, pieces):
    count, layers, rows, lanes = blocks.shape
    total = count * rows
    return pl.pallas_call(
        lines_kernel,
        grid=(layers,),
        in_specs=[
            pl.BlockSpec((count, 1, rows, lanes), lambda i: (0, i, 0, 0)),
        ]
        + [pl.BlockSpec((total, total), lambda i: (0, 0)) for _ in tables],
        out_specs=pl.BlockSpec((pieces, 1, total // pieces, lanes), lambda i: (0, i, 0, 0)),
        out_shape=jax.ShapeDtypeStruct((pieces, layers, total // pieces, lanes), F32),
        compiler_params=params(),
    )(blocks, *tables)


def forward_kernel(x_ref, s_high, s_low, k_high, k_low, lam_ref, ey_ref, ends_ref, b_ref, fl_ref):
    total_z, rows, lanes = x_ref.shape
    value = x_ref[...].reshape(total_z * rows, lanes)
    spectrum = table_left(k_high, k_low, table_right(value, s_high, s_low))
    b_ref[...] = spectrum.reshape(b_ref.shape)
    local = spectrum / (lam_ref[0] + ey_ref[...])
    fl_ref[0] = lax.dot_general(
        ends_ref[...],
        local,
        (((1,), (1,)), ((), ())),
        precision=lax.Precision.HIGHEST,
        preferred_element_type=F32,
    )


def backward_kernel(b_ref, ab_ref, s_ref, k_ref, lam_ref, ey_ref, ends_ref, u_ref):
    total_z, rows, lanes = b_ref.shape
    spectrum = b_ref[...].reshape(total_z * rows, lanes)
    ends = lax.dot_general(
        ab_ref[0],
        ends_ref[...],
        (((0,), (0,)), ((), ())),
        precision=lax.Precision.HIGHEST,
        preferred_element_type=F32,
    )
    solved = (spectrum + ends) / (lam_ref[0] + ey_ref[...])
    u_ref[...] = full(k_ref[...], full(solved, s_ref[...])).reshape(u_ref.shape)


def solve(source, sets, sets_z):
    local_z, local_x, local_y = source.shape
    nx, ny, nz = lax.axis_size("gx"), lax.axis_size("gy"), lax.axis_size("gz")
    total_x, total_z = local_x * nx, local_z * nz
    group = nx * nz
    layers = local_z // nx
    part_x = total_x // group
    tiles = part_x // 8
    pair_rows = total_z * 8
    chunk = lax.axis_index("gz") * nx + lax.axis_index("gx")

    e_x = 4.0 * np.sin(np.pi * (np.arange(total_x) + 1) / (2 * total_x)) ** 2
    e_z = 4.0 * np.sin(np.pi * np.arange(total_z) / (2 * total_z)) ** 2
    lam = ANISOTROPY * e_z[:, None] + e_x[None, :]
    lam = lam.reshape(total_z, group, tiles, 8).transpose(1, 2, 0, 3).reshape(group, tiles, pair_rows)
    theta = np.log1p(lam / 2 + np.sqrt(lam + lam * lam / 4))
    whole = np.expm1(-2 * (local_y + 1) * theta)
    alpha = np.exp(-theta) * np.expm1(-2 * local_y * theta) / whole
    beta = np.exp(-local_y * theta) * np.expm1(-2 * theta) / whole
    response = [alpha - beta * beta / (1 + alpha)]
    inverse = [1 / (1 + alpha)]
    for _ in range(1, ny):
        inverse.append(1 / (1 - alpha * response[-1]))
        response.append(alpha + beta * beta * response[-1] * inverse[-1])
    closing = 1 / (1 + response[-1])

    def mine(table):
        return lax.dynamic_index_in_dim(jnp.asarray(table, F32), chunk, 0, keepdims=False)

    basis = sine_whole(local_y)
    e_y = 4.0 * np.sin(np.pi * (np.arange(local_y) + 1) / (2 * (local_y + 1))) ** 2
    ends = np.zeros((8, local_y))
    ends[0], ends[1] = basis[:, 0], basis[:, -1]
    ends = jnp.asarray(ends, F32)
    ey = jnp.asarray(e_y[None, :], F32)
    lam_rows = mine(lam)[:, :, None]
    s_high, s_low = split_table(basis)
    cosine = np.kron(cosine_half(total_z), np.eye(8))
    forward_z = split_table(2.0 * cosine)
    backward_z = jnp.asarray(cosine.T, F32)

    together = lax.optimization_barrier
    source, first_z = together((source, sets_z[0]))
    sets_z = [first_z] + sets_z[1:]
    blocks = source.reshape(nx, layers, local_x, local_y)
    blocks = lax.all_to_all(blocks, "gx", 0, 0)
    blocks, sets_z = together((blocks, sets_z))
    sets_x = [x_halo(a, *z) for a, z in zip(sets, sets_z)]
    sine_x = sine_half(total_x)
    blocks = x_lines(blocks, split_table(sine_x), group)
    blocks, sets_x = together((blocks, sets_x))
    packs = [y_pack(a, *z, *x) for a, z, x in zip(sets, sets_z, sets_x)]
    blocks = lax.all_to_all(blocks, ("gz", "gx"), 0, 0)
    blocks, packs = together((blocks, packs))
    sets_y = [shift_pair(*pack, "gy") for pack in packs]
    columns = blocks.reshape(total_z, part_x, local_y)

    cube = pl.BlockSpec((total_z, 8, local_y), lambda i: (0, i, 0))
    small = pl.BlockSpec((1, 8, pair_rows), lambda i: (i, 0, 0))
    tables = [
        pl.BlockSpec((local_y, local_y), lambda i: (0, 0)),
        pl.BlockSpec((local_y, local_y), lambda i: (0, 0)),
        pl.BlockSpec((pair_rows, pair_rows), lambda i: (0, 0)),
        pl.BlockSpec((pair_rows, pair_rows), lambda i: (0, 0)),
        pl.BlockSpec((1, pair_rows, 1), lambda i: (i, 0, 0)),
        pl.BlockSpec((1, local_y), lambda i: (0, 0)),
        pl.BlockSpec((8, local_y), lambda i: (0, 0)),
    ]
    spectrum, edge = pl.pallas_call(
        forward_kernel,
        grid=(tiles,),
        in_specs=[cube] + tables,
        out_specs=[cube, small],
        out_shape=[
            jax.ShapeDtypeStruct(columns.shape, F32),
            jax.ShapeDtypeStruct((tiles, 8, pair_rows), F32),
        ],
        compiler_params=params(),
    )(columns, s_high, s_low, *forward_z, lam_rows, ey, ends)

    every = lax.all_gather(edge[:, :2], "gy")
    al, be = mine(alpha), mine(beta)
    re = [mine(r) for r in response]
    inv = [mine(r) for r in inverse]
    first_in = [every[p, :, 0] for p in range(ny)]
    last_in = [every[p, :, 1] for p in range(ny)]
    carried = [last_in[0] - be * first_in[0] * inv[0]]
    for p in range(1, ny):
        prior = carried[-1]
        carried.append(
            last_in[p] + be * (prior + re[p - 1] * (first_in[p] + al * prior) * inv[p])
        )
    first, last = [None] * ny, [None] * ny
    last[ny - 1] = carried[ny - 1] * mine(closing)
    above = -last[ny - 1]
    for p in range(ny - 1, -1, -1):
        if p < ny - 1:
            last[p] = carried[p] + re[p] * above
        if p > 0:
            first[p] = (first_in[p] + al * carried[p - 1] + be * above) * inv[p]
        else:
            first[p] = (first_in[p] + be * above) * inv[p]
        above = first[p]
    below = jnp.stack([-first[0]] + last[:-1])
    above = jnp.stack(first[1:] + [-last[-1]])
    place = lax.axis_index("gy")
    below = lax.dynamic_index_in_dim(below, place, 0, keepdims=False)
    above = lax.dynamic_index_in_dim(above, place, 0, keepdims=False)
    sides = jnp.stack([below, above] + [jnp.zeros_like(below)] * 6, 1)

    columns = pl.pallas_call(
        backward_kernel,
        grid=(tiles,),
        in_specs=[cube, small, tables[0], tables[2]] + tables[4:],
        out_specs=cube,
        out_shape=jax.ShapeDtypeStruct(columns.shape, F32),
        compiler_params=params(),
    )(spectrum, sides, jnp.asarray(basis, F32), backward_z, lam_rows, ey, ends)

    blocks = columns.reshape(group, layers, part_x, local_y)
    blocks = lax.all_to_all(blocks, ("gz", "gx"), 0, 0)
    blocks, sets_y = together((blocks, sets_y))
    blocks = x_lines(blocks, (jnp.asarray(sine_x.T, F32),), nx)
    blocks = lax.all_to_all(blocks, "gx", 0, 0)
    return blocks.reshape(local_z, local_x, local_y), [
        tuple(z) + tuple(x) + tuple(y) for z, x, y in zip(sets_z, sets_x, sets_y)
    ]


def shift_pair(low_part, high_part, axis):
    count = lax.axis_size(axis)
    up = [(i, i + 1) for i in range(count - 1)]
    down = [(target, source) for source, target in up]
    return lax.ppermute(high_part, axis, up), lax.ppermute(low_part, axis, down)


def pack_kernel(groups, span, *refs):
    count = len(groups)
    firsts, finals = refs[:count], refs[count : 2 * count]
    zlf, zll, zhf, zhl, xlf, xll, xhf, xhl, lo_ref, hi_ref = refs[2 * count :]
    step = pl.program_id(0)
    depth = pl.num_programs(0) * span
    rows = firsts[0].shape[2]
    lane = lax.broadcasted_iota(jnp.int32, (1, LANES), 1)

    def packed(k, first, final, old):
        keep = (lane >= W * k) & (lane < W * k + W)
        low = jnp.where(keep, pltpu.roll(first, lax.rem(W * k, LANES), 1), old[0])
        high = jnp.where(keep, pltpu.roll(final, lax.rem(W * k + W, LANES), 1), old[1])
        return low, high

    inner = slice(RX, RX + rows)

    @pl.when(step == 0)
    def _():
        for field in range(sum(groups)):
            for begin, first, final in ((0, xlf, xll), (RX + rows, xhf, xhl)):
                old = (jnp.zeros((RX, LANES), F32),) * 2
                for k in range(first.shape[1]):
                    old = packed(jnp.int32(k), first[field, k], final[field, k], old)
                lo_ref[field, begin : begin + RX, :] = old[0]
                hi_ref[field, begin : begin + RX, :] = old[1]
            old = (jnp.zeros((rows, LANES), F32),) * 2
            for k in range(W):
                old = packed(jnp.int32(k), zlf[field, k], zll[field, k], old)
                old = packed(W + depth + k, zhf[field, k], zhl[field, k], old)
            lo_ref[field, inner, :] = old[0]
            hi_ref[field, inner, :] = old[1]

    field = 0
    for at, size in enumerate(groups):
        for index in range(size):
            old = (lo_ref[field, inner, :], hi_ref[field, inner, :])
            for j in range(span):
                old = packed(
                    W + step * span + j, firsts[at][index, j], finals[at][index, j], old
                )
            lo_ref[field, inner, :] = old[0]
            hi_ref[field, inner, :] = old[1]
            field += 1


def joined(arrays, pick):
    parts = [pick(a) for a in arrays]
    return parts[0] if len(parts) == 1 else jnp.concatenate(parts, 0)


def z_halo(arrays, after=None):
    local_z = arrays[0].shape[1]
    first = joined(arrays, lambda a: a[:, :W])
    final = joined(arrays, lambda a: a[:, local_z - W :])
    if after is not None:
        first, final, _ = lax.optimization_barrier((first, final, after))
    return shift_pair(first, final, "gz")


def x_halo(arrays, z_low, z_high):
    local_x = arrays[0].shape[2]

    def rows(begin):
        cut = lambda a: a[:, :, begin : begin + RX]
        return jnp.concatenate([cut(z_low), joined(arrays, cut), cut(z_high)], 1)

    return shift_pair(rows(0), rows(local_x - RX), "gx")


def y_pack(arrays, z_low, z_high, x_low, x_high):
    local_z, local_x, local_y = arrays[0].shape[1:]
    groups = tuple(a.shape[0] for a in arrays)
    fields = sum(groups)
    final = local_y // LANES - 1
    span = 8

    def edge(shape, at):
        return pl.BlockSpec(shape[:3] + (LANES,), lambda k: (0, 0, 0, at))

    def part(size, at):
        return pl.BlockSpec((size, span, local_x, LANES), lambda k: (0, k, 0, at))

    specs = [part(g, 0) for g in groups] + [part(g, final) for g in groups]
    operands = list(arrays) * 2
    for array in (z_low, z_high, x_low, x_high):
        specs += [edge(array.shape, 0), edge(array.shape, final)]
        operands += [array, array]
    shape = (fields, local_x + 2 * RX, LANES)
    return pl.pallas_call(
        functools.partial(pack_kernel, groups, span),
        grid=(local_z // span,),
        in_specs=specs,
        out_specs=[pl.BlockSpec(shape, lambda k: (0, 0, 0))] * 2,
        out_shape=[jax.ShapeDtypeStruct(shape, F32)] * 2,
        compiler_params=params(),
    )(*operands)


def halos(arrays):
    z_part = z_halo(arrays)
    x_part = x_halo(arrays, *z_part)
    return z_part + x_part + shift_pair(*y_pack(arrays, *z_part, *x_part), "gy")


def halo_specs(fields, local_z, local_x, local_y, plane_of):
    return [
        pl.BlockSpec(
            (fields, 1, local_x, local_y), lambda k: (0, jnp.minimum(plane_of(k), W - 1), 0, 0)
        ),
        pl.BlockSpec(
            (fields, 1, local_x, local_y),
            lambda k: (0, jnp.maximum(plane_of(k) - W - local_z, 0), 0, 0),
        ),
        pl.BlockSpec((fields, 1, RX, local_y), lambda k: (0, plane_of(k), 0, 0)),
        pl.BlockSpec((fields, 1, RX, local_y), lambda k: (0, plane_of(k), 0, 0)),
        pl.BlockSpec((fields, local_x + 2 * RX, LANES), lambda k: (0, 0, 0)),
        pl.BlockSpec((fields, local_x + 2 * RX, LANES), lambda k: (0, 0, 0)),
    ]


def assemble(k, local_z, mains, halo, put):
    z_low, z_high, x_low, x_high, y_low, y_high = halo
    local_x, local_y = z_low.shape[2:]
    every = slice(LEAD, LEAD + local_x + 2 * RX)
    inner = slice(LEAD + RX, LEAD + RX + local_x)
    wide = slice(0, local_y)
    lane = lax.broadcasted_iota(jnp.int32, (1, LANES), 1)
    up = lax.rem(2 * LANES - W * k, LANES)
    down = lax.rem(2 * LANES - W * k - W, LANES)
    field = 0
    for main in mains:
        for index in range(main.shape[0]):

            @pl.when((k >= W) & (k < W + local_z))
            def _():
                put(field, inner, wide, main[index, 0])

            @pl.when(k < W)
            def _():
                put(field, inner, wide, z_low[field, 0])

            @pl.when(k >= W + local_z)
            def _():
                put(field, inner, wide, z_high[field, 0])

            put(field, slice(LEAD, LEAD + RX), wide, x_low[field, 0])
            put(field, slice(inner.stop, inner.stop + RX), wide, x_high[field, 0])
            put(
                field,
                every,
                slice(local_y, local_y + LANES),
                jnp.where(
                    lane < LANES // 2,
                    pltpu.roll(y_high[field], up, 1),
                    pltpu.roll(y_low[field], down, 1),
                ),
            )
            field += 1


def next_y(value):
    return pltpu.roll(value, value.shape[1] - 1, 1)


def prev_y(value):
    return pltpu.roll(value, 1, 1)


def next_x(value, after):
    row = lax.broadcasted_iota(jnp.int32, value.shape, 0)
    return pltpu.roll(jnp.where(row == 0, after, value), 7, 0)


def prev_x(value, before):
    row = lax.broadcasted_iota(jnp.int32, value.shape, 0)
    return pltpu.roll(jnp.where(row == 7, before, value), 1, 0)


def edge_kernel(span, first, last, wind, lo_ref, hi_ref):
    step = pl.program_id(0)
    lane = lax.broadcasted_iota(jnp.int32, (1, LANES), 1)

    @pl.when(step == 0)
    def _():
        lo_ref[...] = jnp.zeros_like(lo_ref)
        hi_ref[...] = jnp.zeros_like(hi_ref)

    low, high = lo_ref[...], hi_ref[...]
    for j in range(span):
        k = step * span + j
        keep = lane == k
        low = jnp.where(keep, pltpu.roll(first[0, j], k, 1), low)
        flux = wind[0, j] * last[0, j]
        high = jnp.where(keep, pltpu.roll(flux, lax.rem(k + 1, LANES), 1), high)
    lo_ref[...] = low
    hi_ref[...] = high


def face_edges(wind, opened):
    local_z, local_x, local_y = wind.shape[1:]
    span = 8
    final = local_y // LANES - 1
    block = (1, span, local_x, LANES)
    shape = jax.ShapeDtypeStruct((local_x, LANES), F32)
    first_y, last_y = pl.pallas_call(
        functools.partial(edge_kernel, span),
        grid=(local_z // span,),
        in_specs=[
            pl.BlockSpec(block, lambda k: (0, k, 0, 0)),
            pl.BlockSpec(block, lambda k: (0, k, 0, final)),
            pl.BlockSpec(block, lambda k: (1, k, 0, final)),
        ],
        out_specs=[pl.BlockSpec((local_x, LANES), lambda k: (0, 0))] * 2,
        out_shape=[shape, shape],
        compiler_params=params(),
    )(opened, opened, wind)
    z_pair = shift_pair(opened[0, 0], wind[2, -1] * opened[0, -1], "gz")
    last_x = slice(local_x - 1, local_x)
    x_pair = shift_pair(opened[0, :, :1], wind[0, :, last_x] * opened[0, :, last_x], "gx")
    return z_pair + x_pair + shift_pair(first_y, last_y, "gy")


def divergence_kernel(wind, opened, over, z_low, z_high, x_low, x_high, y_low, y_high, out, face_z):
    k, depth = pl.program_id(0), pl.num_programs(0)
    local_x, local_y = out.shape[1:]
    lane = lax.broadcasted_iota(jnp.int32, (1, LANES), 1)
    before = None
    for i in range(local_x // 8):
        rows = slice(8 * i, 8 * i + 8)
        cells = opened[0, 0, rows, :]
        if i < local_x // 8 - 1:
            after = opened[0, 0, 8 * i + 8 : 8 * i + 16, :]
        else:
            after = jnp.broadcast_to(x_high[0], cells.shape)
        if before is None:
            before = jnp.broadcast_to(x_low[0] * cells[0:1], cells.shape)
        flux_x = wind[0, 0, rows, :] * (cells * next_x(cells, after))
        right = pltpu.roll(y_high[rows, :], lax.rem(2 * LANES - 1 - k, LANES), 1)
        left = pltpu.roll(y_low[rows, :], lax.rem(LANES - k, LANES), 1)
        beside = next_y(cells)
        cut = local_y - LANES
        tail = jnp.where(lane == LANES - 1, right, beside[:, cut:])
        beside = tail if cut == 0 else jnp.concatenate([beside[:, :cut], tail], 1)
        flux_y = wind[1, 0, rows, :] * (cells * beside)
        back = prev_y(flux_y)
        head = jnp.where(lane == 0, left * cells[:, :LANES], back[:, :LANES])
        back = head if cut == 0 else jnp.concatenate([head, back[:, LANES:]], 1)
        above = jnp.where(k == depth - 1, z_high[rows, :], over[0, 0, rows, :])
        flux_z = wind[2, 0, rows, :] * (cells * above)
        below = jnp.where(k == 0, z_low[rows, :] * cells, face_z[rows, :])
        out[0, rows, :] = (flux_x - prev_x(flux_x, before)) + (flux_y - back) + (flux_z - below)
        face_z[rows, :] = flux_z
        before = flux_x


def divergence(wind, opened, edges):
    local_z, local_x, local_y = wind.shape[1:]
    plane = pl.BlockSpec((local_x, local_y), lambda k: (0, 0))
    line = pl.BlockSpec((1, 1, local_y), lambda k: (k, 0, 0))
    pack = pl.BlockSpec((local_x, LANES), lambda k: (0, 0))
    one = (1, 1, local_x, local_y)
    return pl.pallas_call(
        divergence_kernel,
        grid=(local_z,),
        in_specs=[
            pl.BlockSpec((3, 1, local_x, local_y), lambda k: (0, k, 0, 0)),
            pl.BlockSpec(one, lambda k: (0, k, 0, 0)),
            pl.BlockSpec(one, lambda k: (0, jnp.minimum(k + 1, local_z - 1), 0, 0)),
            plane,
            plane,
            line,
            line,
            pack,
            pack,
        ],
        out_specs=pl.BlockSpec((1, local_x, local_y), lambda k: (k, 0, 0)),
        out_shape=jax.ShapeDtypeStruct((local_z, local_x, local_y), F32),
        scratch_shapes=[pltpu.VMEM((local_x, local_y), F32)],
        compiler_params=params(),
    )(wind, opened, opened, *edges)


def limiter(demand, supply):
    binding = demand > supply
    return jnp.where(binding, supply / jnp.where(binding, demand, 1.0), 1.0)


def transport_kernel(local_z, scalar_count, *refs):
    scal, sc_halo = refs[0], refs[1:7]
    wind, opened, wi_halo = refs[7], refs[8], refs[9:15]
    mult, mu_halo = refs[15], refs[16:22]
    factor, wind_out, out = refs[22:25]
    speed, cell, kept = refs[25], refs[26], refs[27:]
    conc, trial, upper, lower, anti, ratio, low_z, lim_z, edge, result = (
        kept[at * scalar_count : (at + 1) * scalar_count] for at in range(10)
    )
    k = pl.program_id(0)
    local_x, local_y = out.shape[2:]
    lanes = local_y + LANES
    count = local_x // 8 + 2
    s1, s2, s3 = (lax.rem(k + 3 - d, 3) for d in range(1, 4))
    now, old = lax.rem(k, 2), lax.rem(k + 1, 2)

    def put_scalar(field, rows, wide, value):
        conc[field][now, rows, wide] = value

    def put_wind(field, rows, wide, value):
        cell[now, field, rows, wide] = value

    def put_mult(field, rows, wide, value):
        cell[now, 4, rows, wide] = value

    assemble(k, local_z, (scal,), sc_halo, put_scalar)
    assemble(k, local_z, (wind, opened), wi_halo, put_wind)
    assemble(k, local_z, (mult,), mu_halo, put_mult)

    def chunk(i):
        return pl.ds(pl.multiple_of(i * 8, 8), 8)

    def keep_ratios(s, mid, up_new, down_new):
        ratio[s][now, 0, mid, :] = up_new
        ratio[s][now, 1, mid, :] = down_new

    def keep(s, here, antis, lows, t_new, u_new, l_new):
        low_z[s][here, :] = lows[2]
        edge[s][0] = lows[0]
        trial[s][s1, here, :] = t_new
        upper[s][s1, here, :] = u_new
        lower[s][s1, here, :] = l_new
        for d in range(3):
            anti[s][s1, d, here, :] = antis[d]

    def limit(a, up_here, down_here, up_next, down_next):
        share = jnp.where(
            a >= 0.0, jnp.minimum(up_next, down_here), jnp.minimum(up_here, down_next)
        )
        return share * a

    def column(stages, i, _):
        last, mid, here, after = (chunk(i + d) for d in range(4))

        cells, multiplier = cell[old, 3, here, :], cell[old, 4, here, :]
        neighbours = (
            (next_x(cells, cell[old, 3, after, :]), next_x(multiplier, cell[old, 4, after, :])),
            (next_y(cells), next_y(multiplier)),
            (cell[now, 3, here, :], cell[now, 4, here, :]),
        )
        speeds, halves, sizes = [], [], []
        for d in range(3):
            open_next, mult_next = neighbours[d]
            face = cells * open_next
            value = (cell[old, d, here, :] * face + GAINS[d] * (mult_next - multiplier)) * face
            speeds.append(value)
            halves.append((0.5 * TIME_STEP) * value)
            sizes.append(jnp.abs(halves[-1]))
        for d in range(3):
            speed[d, here, :] = speeds[d][:, :local_y]

        for s in range(scalar_count):
            c = conc[s][old, here, :]
            downwind = (next_x(c, conc[s][old, after, :]), next_y(c), conc[s][now, here, :])
            antis, lows = [], []
            for d in range(3):
                a = sizes[d] * (downwind[d] - c)
                antis.append(a)
                lows.append(halves[d] * (downwind[d] + c) - a)
            change = (lows[0] - prev_x(lows[0], edge[s][0])) + (lows[1] - prev_y(lows[1]))
            t_new = c - (change + (lows[2] - low_z[s][here, :]))
            u_new, l_new = jnp.maximum(c, t_new), jnp.minimum(c, t_new)

            new = (here, antis, lows, t_new, u_new, l_new)
            if stages == 1:
                keep(s, *new)
                continue

            u, l = upper[s][s2, mid, :], lower[s][s2, mid, :]
            ceiling = jnp.maximum(
                jnp.maximum(u, upper[s][s1, mid, :]),
                jnp.maximum(
                    next_x(u, upper[s][s2, here, :]), prev_x(u, upper[s][s2, last, :])
                ),
            )
            ceiling = jnp.maximum(
                jnp.maximum(ceiling, upper[s][s3, mid, :]), jnp.maximum(next_y(u), prev_y(u))
            )
            bottom = jnp.minimum(
                jnp.minimum(l, lower[s][s1, mid, :]),
                jnp.minimum(
                    next_x(l, lower[s][s2, here, :]), prev_x(l, lower[s][s2, last, :])
                ),
            )
            bottom = jnp.minimum(
                jnp.minimum(bottom, lower[s][s3, mid, :]), jnp.minimum(next_y(l), prev_y(l))
            )
            a_x, a_y, a_z = (anti[s][s2, d, mid, :] for d in range(3))
            befores = (
                prev_x(a_x, anti[s][s2, 0, last, :]),
                prev_y(a_y),
                anti[s][s3, 2, mid, :],
            )
            inflow, outflow = 0.0, 0.0
            for a, b in zip((a_x, a_y, a_z), befores):
                inflow = inflow + (jnp.maximum(b, 0.0) - jnp.minimum(a, 0.0))
                outflow = outflow + (jnp.maximum(a, 0.0) - jnp.minimum(b, 0.0))
            t_mid = trial[s][s2, mid, :]
            up_new = limiter(inflow, ceiling - t_mid)
            down_new = limiter(outflow, t_mid - bottom)

            ratios = (mid, up_new, down_new)
            if stages == 2:
                keep(s, *new)
                keep_ratios(s, *ratios)
                continue

            r_up, r_down = ratio[s][old, 0, last, :], ratio[s][old, 1, last, :]
            own_up, own_down = r_up[:, :local_y], r_down[:, :local_y]
            own = slice(0, local_y)
            limited = (
                limit(
                    anti[s][s3, 0, last, own],
                    own_up,
                    own_down,
                    next_x(own_up, ratio[s][old, 0, mid, own]),
                    next_x(own_down, ratio[s][old, 1, mid, own]),
                ),
                limit(anti[s][s3, 1, last, :], r_up, r_down, next_y(r_up), next_y(r_down)),
                limit(
                    anti[s][s3, 2, last, own],
                    own_up,
                    own_down,
                    ratio[s][now, 0, last, own],
                    ratio[s][now, 1, last, own],
                ),
            )
            moved = limited[0] - prev_x(limited[0], edge[s][1, :, own])
            moved = moved + (limited[1] - prev_y(limited[1]))[:, :local_y]
            moved = moved + (limited[2] - lim_z[s][last, :])
            result[s][last, :] = trial[s][s3, last, own] - moved
            lim_z[s][last, :] = limited[2]
            edge[s][1, :, own] = limited[0]
            keep_ratios(s, *ratios)
            keep(s, *new)
        return 0

    for stages, begin, end in ((1, 1, 4), (2, 4, 5), (3, 5, local_z + 2 * W)):

        @pl.when((k >= begin) & (k < end))
        def _():
            lax.fori_loop(0, count + 1, functools.partial(column, stages), 0)

    inner = slice(LEAD + RX, LEAD + RX + local_x)

    @pl.when((k > W) & (k <= W + local_z))
    def _():
        for d in range(3):
            wind_out[d, 0] = speed[d, inner, :]

    @pl.when(k > 2 * W)
    def _():
        for s in range(scalar_count):
            out[s, 0] = result[s][inner, :]

    @pl.when(k == 2 * W)
    def _():
        for s in range(scalar_count):
            out[s, 0] = result[s][inner, :] * factor[s]


def transport(scalars, sc_halo, wind, opened, wi_halo, mult, mu_halo, factor):
    n, local_z, local_x, local_y = scalars.shape
    same = lambda k: k
    middle = lambda k: (0, jnp.clip(k - W, 0, local_z - 1), 0, 0)
    lanes = local_y + LANES
    rows = local_x + 2 * RX + 2 * LEAD
    plane = (rows, lanes)

    def main(count):
        return [pl.BlockSpec((count, 1, local_x, local_y), middle)]

    def halo(count):
        return halo_specs(count, local_z, local_x, local_y, same)

    return pl.pallas_call(
        functools.partial(transport_kernel, local_z, n),
        grid=(local_z + 2 * W,),
        in_specs=main(n)
        + halo(n)
        + main(3)
        + main(1)
        + halo(4)
        + main(1)
        + halo(1)
        + [pl.BlockSpec((n, local_x, local_y), lambda k: (0, 0, 0))],
        out_specs=[
            pl.BlockSpec(
                (3, 1, local_x, local_y), lambda k: (0, jnp.clip(k - 1 - W, 0, local_z - 1), 0, 0)
            ),
            pl.BlockSpec(
                (n, 1, local_x, local_y), lambda k: (0, jnp.clip(k - 2 * W, 0, local_z - 1), 0, 0)
            ),
        ],
        out_shape=[
            jax.ShapeDtypeStruct((3, local_z, local_x, local_y), F32),
            jax.ShapeDtypeStruct(scalars.shape, F32),
        ],
        scratch_shapes=[pltpu.VMEM((3, rows, local_y), F32), pltpu.VMEM((2, 5) + plane, F32)]
        + [
            pltpu.VMEM(shape, F32)
            for shape in (
                (2,) + plane,
                (3,) + plane,
                (3,) + plane,
                (3,) + plane,
                (3, 3) + plane,
                (2, 2) + plane,
                plane,
                (rows, local_y),
                (2, 8, lanes),
                (rows, local_y),
            )
            for _ in range(n)
        ],
        compiler_params=params(),
    )(scalars, *sc_halo, wind, opened, *wi_halo, mult, *mu_halo, factor)


def ground_factor(surface_flags):
    rates = 1.0 - TIME_STEP * np.asarray(DEPOSIT, np.float32)
    factor = jnp.zeros((len(DEPOSIT),) + surface_flags.shape, F32)
    for surface in range(4):
        column = jnp.asarray(rates[:, surface], F32)[:, None, None]
        factor = factor + jnp.where(surface_flags[None] == surface, column, 0.0)
    return jnp.where(lax.axis_index("gz") == 0, factor, 1.0)


def body(initial_wind, building_mask, surface_flags, scalars):
    opened = (1.0 - building_mask.astype(F32))[None]
    edges = face_edges(initial_wind, opened)
    sets = [(initial_wind, opened), (scalars,)]
    sets_z = [z_halo(arrays, edges[:2]) for arrays in sets]
    source = divergence(initial_wind, opened, edges)
    multiplier, (wind_halo, scalar_halo) = solve(source, sets, sets_z)
    multiplier = multiplier[None]
    mult_halo = halos((multiplier,))
    corrected, transported = transport(
        scalars,
        scalar_halo,
        initial_wind,
        opened,
        wind_halo,
        multiplier,
        mult_halo,
        ground_factor(surface_flags),
    )
    return (corrected, transported)


def solution(mesh):
    in_specs = (
        P(None, "gz", "gx", "gy"),
        P("gz", "gx", "gy"),
        P("gx", "gy"),
        P(None, "gz", "gx", "gy"),
    )
    out_specs = (P(None, "gz", "gx", "gy"), P(None, "gz", "gx", "gy"))
    return jax.shard_map(body, mesh=mesh, in_specs=in_specs, out_specs=out_specs, check_vma=False)
```

```python
import functools
import math

import jax
import jax.numpy as jnp
import ml_dtypes
import numpy as np
from jax import lax
from jax.experimental import pallas as pl
from jax.experimental.pallas import tpu as pltpu
from jax.sharding import PartitionSpec as P

TIME_STEP = 0.2
ANISOTROPY = 4.0
GAINS = (0.5, 0.5, 0.5 * ANISOTROPY)
DEPOSIT = (
    (0.0, 0.25, 0.75, 1.5),
    (0.0, 0.5, 1.0, 2.0),
    (0.1, 0.4, 0.8, 1.6),
    (0.0, 0.15, 1.25, 2.5),
)
W = 3
RX = 8
LEAD = 16
LANES = 128
F32 = jnp.float32
BF16 = jnp.bfloat16
VMEM_LIMIT = 60 * 1024 * 1024


def params():
    return pltpu.CompilerParams(
        dimension_semantics=("arbitrary",), vmem_limit_bytes=VMEM_LIMIT
    )


def sine_half(extent):
    k = np.arange(extent)[:, None]
    n = np.arange(extent)[None, :]
    weight = np.where(k == extent - 1, math.sqrt(1.0 / extent), math.sqrt(2.0 / extent))
    return weight * np.sin(np.pi * ((k + 1) * (2 * n + 1) % (4 * extent)) / (2 * extent))


def cosine_half(extent):
    k = np.arange(extent)[:, None]
    n = np.arange(extent)[None, :]
    weight = np.where(k == 0, math.sqrt(1.0 / extent), math.sqrt(2.0 / extent))
    return weight * np.cos(np.pi * (k * (2 * n + 1) % (4 * extent)) / (2 * extent))


def sine_whole(extent):
    k = np.arange(extent)[:, None] + 1
    n = np.arange(extent)[None, :] + 1
    return math.sqrt(2.0 / (extent + 1)) * np.sin(np.pi * (k * n % (2 * extent + 2)) / (extent + 1))


def split_table(table):
    table = np.asarray(table, np.float32)
    high = table.astype(ml_dtypes.bfloat16)
    low = (table - high.astype(np.float32)).astype(ml_dtypes.bfloat16)
    return jnp.asarray(high), jnp.asarray(low)


def split_value(value):
    high = value.astype(BF16)
    return high, (value - high.astype(F32)).astype(BF16)


def mm(left, right):
    return jnp.dot(left, right, preferred_element_type=F32)


def table_left(high, low, value):
    v_high, v_low = split_value(value)
    return mm(high[...], v_high) + (mm(high[...], v_low) + mm(low[...], v_high))


def table_right(value, high, low):
    v_high, v_low = split_value(value)
    return mm(v_high, high[...]) + (mm(v_low, high[...]) + mm(v_high, low[...]))


def full(left, right):
    return jnp.dot(
        left, right, precision=lax.Precision.HIGHEST, preferred_element_type=F32
    )


def lines_kernel(x_ref, *refs):
    tables, o_ref = refs[:-1], refs[-1]
    count, _, rows, lanes = x_ref.shape
    value = x_ref[...].reshape(count * rows, lanes)
    if len(tables) == 2:
        result = table_left(*tables, value)
    else:
        result = full(tables[0][...], value)
    o_ref[...] = result.reshape(o_ref.shape)


def x_lines(blocks, tables, pieces):
    count, layers, rows, lanes = blocks.shape
    total = count * rows
    return pl.pallas_call(
        lines_kernel,
        grid=(layers,),
        in_specs=[
            pl.BlockSpec((count, 1, rows, lanes), lambda i: (0, i, 0, 0)),
        ]
        + [pl.BlockSpec((total, total), lambda i: (0, 0)) for _ in tables],
        out_specs=pl.BlockSpec((pieces, 1, total // pieces, lanes), lambda i: (0, i, 0, 0)),
        out_shape=jax.ShapeDtypeStruct((pieces, layers, total // pieces, lanes), F32),
        compiler_params=params(),
    )(blocks, *tables)


def forward_kernel(x_ref, s_high, s_low, k_high, k_low, lam_ref, ey_ref, ends_ref, b_ref, fl_ref):
    total_z, rows, lanes = x_ref.shape
    value = x_ref[...].reshape(total_z * rows, lanes)
    spectrum = table_left(k_high, k_low, table_right(value, s_high, s_low))
    b_ref[...] = spectrum.reshape(b_ref.shape)
    local = spectrum / (lam_ref[0] + ey_ref[...])
    fl_ref[0] = lax.dot_general(
        ends_ref[...],
        local,
        (((1,), (1,)), ((), ())),
        precision=lax.Precision.HIGHEST,
        preferred_element_type=F32,
    )


def backward_kernel(b_ref, ab_ref, s_ref, k_ref, lam_ref, ey_ref, ends_ref, u_ref):
    total_z, rows, lanes = b_ref.shape
    spectrum = b_ref[...].reshape(total_z * rows, lanes)
    ends = lax.dot_general(
        ab_ref[0],
        ends_ref[...],
        (((0,), (0,)), ((), ())),
        precision=lax.Precision.HIGHEST,
        preferred_element_type=F32,
    )
    solved = (spectrum + ends) / (lam_ref[0] + ey_ref[...])
    u_ref[...] = full(k_ref[...], full(solved, s_ref[...])).reshape(u_ref.shape)


def solve(source, sets, sets_z):
    local_z, local_x, local_y = source.shape
    nx, ny, nz = lax.axis_size("gx"), lax.axis_size("gy"), lax.axis_size("gz")
    total_x, total_z = local_x * nx, local_z * nz
    group = nx * nz
    layers = local_z // nx
    part_x = total_x // group
    tiles = part_x // 8
    pair_rows = total_z * 8
    chunk = lax.axis_index("gz") * nx + lax.axis_index("gx")

    e_x = 4.0 * np.sin(np.pi * (np.arange(total_x) + 1) / (2 * total_x)) ** 2
    e_z = 4.0 * np.sin(np.pi * np.arange(total_z) / (2 * total_z)) ** 2
    lam = ANISOTROPY * e_z[:, None] + e_x[None, :]
    lam = lam.reshape(total_z, group, tiles, 8).transpose(1, 2, 0, 3).reshape(group, tiles, pair_rows)
    theta = np.log1p(lam / 2 + np.sqrt(lam + lam * lam / 4))
    whole = np.expm1(-2 * (local_y + 1) * theta)
    alpha = np.exp(-theta) * np.expm1(-2 * local_y * theta) / whole
    beta = np.exp(-local_y * theta) * np.expm1(-2 * theta) / whole
    response = [alpha - beta * beta / (1 + alpha)]
    inverse = [1 / (1 + alpha)]
    for _ in range(1, ny):
        inverse.append(1 / (1 - alpha * response[-1]))
        response.append(alpha + beta * beta * response[-1] * inverse[-1])
    closing = 1 / (1 + response[-1])

    def mine(table):
        return lax.dynamic_index_in_dim(jnp.asarray(table, F32), chunk, 0, keepdims=False)

    basis = sine_whole(local_y)
    e_y = 4.0 * np.sin(np.pi * (np.arange(local_y) + 1) / (2 * (local_y + 1))) ** 2
    ends = np.zeros((8, local_y))
    ends[0], ends[1] = basis[:, 0], basis[:, -1]
    ends = jnp.asarray(ends, F32)
    ey = jnp.asarray(e_y[None, :], F32)
    lam_rows = mine(lam)[:, :, None]
    s_high, s_low = split_table(basis)
    cosine = np.kron(cosine_half(total_z), np.eye(8))
    forward_z = split_table(2.0 * cosine)
    backward_z = jnp.asarray(cosine.T, F32)

    together = lax.optimization_barrier
    source, first_z = together((source, sets_z[0]))
    sets_z = [first_z] + sets_z[1:]
    blocks = source.reshape(nx, layers, local_x, local_y)
    blocks = lax.all_to_all(blocks, "gx", 0, 0)
    blocks, sets_z = together((blocks, sets_z))
    sets_x = [x_halo(a, *z) for a, z in zip(sets, sets_z)]
    sine_x = sine_half(total_x)
    blocks = x_lines(blocks, split_table(sine_x), group)
    blocks, sets_x = together((blocks, sets_x))
    packs = [y_pack(a, *z, *x) for a, z, x in zip(sets, sets_z, sets_x)]
    blocks = lax.all_to_all(blocks, ("gz", "gx"), 0, 0)
    blocks, packs = together((blocks, packs))
    sets_y = [shift_pair(*pack, "gy") for pack in packs]
    columns = blocks.reshape(total_z, part_x, local_y)

    cube = pl.BlockSpec((total_z, 8, local_y), lambda i: (0, i, 0))
    small = pl.BlockSpec((1, 8, pair_rows), lambda i: (i, 0, 0))
    tables = [
        pl.BlockSpec((local_y, local_y), lambda i: (0, 0)),
        pl.BlockSpec((local_y, local_y), lambda i: (0, 0)),
        pl.BlockSpec((pair_rows, pair_rows), lambda i: (0, 0)),
        pl.BlockSpec((pair_rows, pair_rows), lambda i: (0, 0)),
        pl.BlockSpec((1, pair_rows, 1), lambda i: (i, 0, 0)),
        pl.BlockSpec((1, local_y), lambda i: (0, 0)),
        pl.BlockSpec((8, local_y), lambda i: (0, 0)),
    ]
    spectrum, edge = pl.pallas_call(
        forward_kernel,
        grid=(tiles,),
        in_specs=[cube] + tables,
        out_specs=[cube, small],
        out_shape=[
            jax.ShapeDtypeStruct(columns.shape, F32),
            jax.ShapeDtypeStruct((tiles, 8, pair_rows), F32),
        ],
        compiler_params=params(),
    )(columns, s_high, s_low, *forward_z, lam_rows, ey, ends)

    every = lax.all_gather(edge[:, :2], "gy")
    al, be = mine(alpha), mine(beta)
    re = [mine(r) for r in response]
    inv = [mine(r) for r in inverse]
    first_in = [every[p, :, 0] for p in range(ny)]
    last_in = [every[p, :, 1] for p in range(ny)]
    carried = [last_in[0] - be * first_in[0] * inv[0]]
    for p in range(1, ny):
        prior = carried[-1]
        carried.append(
            last_in[p] + be * (prior + re[p - 1] * (first_in[p] + al * prior) * inv[p])
        )
    first, last = [None] * ny, [None] * ny
    last[ny - 1] = carried[ny - 1] * mine(closing)
    above = -last[ny - 1]
    for p in range(ny - 1, -1, -1):
        if p < ny - 1:
            last[p] = carried[p] + re[p] * above
        if p > 0:
            first[p] = (first_in[p] + al * carried[p - 1] + be * above) * inv[p]
        else:
            first[p] = (first_in[p] + be * above) * inv[p]
        above = first[p]
    below = jnp.stack([-first[0]] + last[:-1])
    above = jnp.stack(first[1:] + [-last[-1]])
    place = lax.axis_index("gy")
    below = lax.dynamic_index_in_dim(below, place, 0, keepdims=False)
    above = lax.dynamic_index_in_dim(above, place, 0, keepdims=False)
    sides = jnp.stack([below, above] + [jnp.zeros_like(below)] * 6, 1)

    columns = pl.pallas_call(
        backward_kernel,
        grid=(tiles,),
        in_specs=[cube, small, tables[0], tables[2]] + tables[4:],
        out_specs=cube,
        out_shape=jax.ShapeDtypeStruct(columns.shape, F32),
        compiler_params=params(),
    )(spectrum, sides, jnp.asarray(basis, F32), backward_z, lam_rows, ey, ends)

    blocks = columns.reshape(group, layers, part_x, local_y)
    blocks = lax.all_to_all(blocks, ("gz", "gx"), 0, 0)
    blocks, sets_y = together((blocks, sets_y))
    blocks = x_lines(blocks, (jnp.asarray(sine_x.T, F32),), nx)
    blocks = lax.all_to_all(blocks, "gx", 0, 0)
    return blocks.reshape(local_z, local_x, local_y), [
        tuple(z) + tuple(x) + tuple(y) for z, x, y in zip(sets_z, sets_x, sets_y)
    ]


def shift_pair(low_part, high_part, axis):
    count = lax.axis_size(axis)
    up = [(i, i + 1) for i in range(count - 1)]
    down = [(target, source) for source, target in up]
    return lax.ppermute(high_part, axis, up), lax.ppermute(low_part, axis, down)


def pack_kernel(groups, span, *refs):
    count = len(groups)
    firsts, finals = refs[:count], refs[count : 2 * count]
    zlf, zll, zhf, zhl, xlf, xll, xhf, xhl, lo_ref, hi_ref = refs[2 * count :]
    step = pl.program_id(0)
    depth = pl.num_programs(0) * span
    rows = firsts[0].shape[2]
    lane = lax.broadcasted_iota(jnp.int32, (1, LANES), 1)

    def packed(k, first, final, old):
        keep = (lane >= W * k) & (lane < W * k + W)
        low = jnp.where(keep, pltpu.roll(first, lax.rem(W * k, LANES), 1), old[0])
        high = jnp.where(keep, pltpu.roll(final, lax.rem(W * k + W, LANES), 1), old[1])
        return low, high

    inner = slice(RX, RX + rows)

    @pl.when(step == 0)
    def _():
        for field in range(sum(groups)):
            for begin, first, final in ((0, xlf, xll), (RX + rows, xhf, xhl)):
                old = (jnp.zeros((RX, LANES), F32),) * 2
                for k in range(first.shape[1]):
                    old = packed(jnp.int32(k), first[field, k], final[field, k], old)
                lo_ref[field, begin : begin + RX, :] = old[0]
                hi_ref[field, begin : begin + RX, :] = old[1]
            old = (jnp.zeros((rows, LANES), F32),) * 2
            for k in range(W):
                old = packed(jnp.int32(k), zlf[field, k], zll[field, k], old)
                old = packed(W + depth + k, zhf[field, k], zhl[field, k], old)
            lo_ref[field, inner, :] = old[0]
            hi_ref[field, inner, :] = old[1]

    field = 0
    for at, size in enumerate(groups):
        for index in range(size):
            old = (lo_ref[field, inner, :], hi_ref[field, inner, :])
            for j in range(span):
                old = packed(
                    W + step * span + j, firsts[at][index, j], finals[at][index, j], old
                )
            lo_ref[field, inner, :] = old[0]
            hi_ref[field, inner, :] = old[1]
            field += 1


def joined(arrays, pick):
    parts = [pick(a) for a in arrays]
    return parts[0] if len(parts) == 1 else jnp.concatenate(parts, 0)


def z_halo(arrays, after=None):
    local_z = arrays[0].shape[1]
    first = joined(arrays, lambda a: a[:, :W])
    final = joined(arrays, lambda a: a[:, local_z - W :])
    if after is not None:
        first, final, _ = lax.optimization_barrier((first, final, after))
    return shift_pair(first, final, "gz")


def x_halo(arrays, z_low, z_high):
    local_x = arrays[0].shape[2]

    def rows(begin):
        cut = lambda a: a[:, :, begin : begin + RX]
        return jnp.concatenate([cut(z_low), joined(arrays, cut), cut(z_high)], 1)

    return shift_pair(rows(0), rows(local_x - RX), "gx")


def y_pack(arrays, z_low, z_high, x_low, x_high):
    local_z, local_x, local_y = arrays[0].shape[1:]
    groups = tuple(a.shape[0] for a in arrays)
    fields = sum(groups)
    final = local_y // LANES - 1
    span = 8

    def edge(shape, at):
        return pl.BlockSpec(shape[:3] + (LANES,), lambda k: (0, 0, 0, at))

    def part(size, at):
        return pl.BlockSpec((size, span, local_x, LANES), lambda k: (0, k, 0, at))

    specs = [part(g, 0) for g in groups] + [part(g, final) for g in groups]
    operands = list(arrays) * 2
    for array in (z_low, z_high, x_low, x_high):
        specs += [edge(array.shape, 0), edge(array.shape, final)]
        operands += [array, array]
    shape = (fields, local_x + 2 * RX, LANES)
    return pl.pallas_call(
        functools.partial(pack_kernel, groups, span),
        grid=(local_z // span,),
        in_specs=specs,
        out_specs=[pl.BlockSpec(shape, lambda k: (0, 0, 0))] * 2,
        out_shape=[jax.ShapeDtypeStruct(shape, F32)] * 2,
        compiler_params=params(),
    )(*operands)


def halos(arrays):
    z_part = z_halo(arrays)
    x_part = x_halo(arrays, *z_part)
    return z_part + x_part + shift_pair(*y_pack(arrays, *z_part, *x_part), "gy")


def halo_specs(fields, local_z, local_x, local_y, plane_of):
    return [
        pl.BlockSpec(
            (fields, 1, local_x, local_y), lambda k: (0, jnp.minimum(plane_of(k), W - 1), 0, 0)
        ),
        pl.BlockSpec(
            (fields, 1, local_x, local_y),
            lambda k: (0, jnp.maximum(plane_of(k) - W - local_z, 0), 0, 0),
        ),
        pl.BlockSpec((fields, 1, RX, local_y), lambda k: (0, plane_of(k), 0, 0)),
        pl.BlockSpec((fields, 1, RX, local_y), lambda k: (0, plane_of(k), 0, 0)),
        pl.BlockSpec((fields, local_x + 2 * RX, LANES), lambda k: (0, 0, 0)),
        pl.BlockSpec((fields, local_x + 2 * RX, LANES), lambda k: (0, 0, 0)),
    ]


def assemble(k, local_z, mains, halo, put):
    z_low, z_high, x_low, x_high, y_low, y_high = halo
    local_x, local_y = z_low.shape[2:]
    every = slice(LEAD, LEAD + local_x + 2 * RX)
    inner = slice(LEAD + RX, LEAD + RX + local_x)
    wide = slice(0, local_y)
    lane = lax.broadcasted_iota(jnp.int32, (1, LANES), 1)
    up = lax.rem(2 * LANES - W * k, LANES)
    down = lax.rem(2 * LANES - W * k - W, LANES)
    field = 0
    for main in mains:
        for index in range(main.shape[0]):

            @pl.when((k >= W) & (k < W + local_z))
            def _():
                put(field, inner, wide, main[index, 0])

            @pl.when(k < W)
            def _():
                put(field, inner, wide, z_low[field, 0])

            @pl.when(k >= W + local_z)
            def _():
                put(field, inner, wide, z_high[field, 0])

            put(field, slice(LEAD, LEAD + RX), wide, x_low[field, 0])
            put(field, slice(inner.stop, inner.stop + RX), wide, x_high[field, 0])
            put(
                field,
                every,
                slice(local_y, local_y + LANES),
                jnp.where(
                    lane < LANES // 2,
                    pltpu.roll(y_high[field], up, 1),
                    pltpu.roll(y_low[field], down, 1),
                ),
            )
            field += 1


def next_y(value):
    return pltpu.roll(value, value.shape[1] - 1, 1)


def prev_y(value):
    return pltpu.roll(value, 1, 1)


def next_x(value, after):
    row = lax.broadcasted_iota(jnp.int32, value.shape, 0)
    return pltpu.roll(jnp.where(row == 0, after, value), 7, 0)


def prev_x(value, before):
    row = lax.broadcasted_iota(jnp.int32, value.shape, 0)
    return pltpu.roll(jnp.where(row == 7, before, value), 1, 0)


def edge_kernel(span, first, last, wind, lo_ref, hi_ref):
    step = pl.program_id(0)
    lane = lax.broadcasted_iota(jnp.int32, (1, LANES), 1)

    @pl.when(step == 0)
    def _():
        lo_ref[...] = jnp.zeros_like(lo_ref)
        hi_ref[...] = jnp.zeros_like(hi_ref)

    low, high = lo_ref[...], hi_ref[...]
    for j in range(span):
        k = step * span + j
        keep = lane == k
        low = jnp.where(keep, pltpu.roll(first[0, j], k, 1), low)
        flux = wind[0, j] * last[0, j]
        high = jnp.where(keep, pltpu.roll(flux, lax.rem(k + 1, LANES), 1), high)
    lo_ref[...] = low
    hi_ref[...] = high


def face_edges(wind, opened):
    local_z, local_x, local_y = wind.shape[1:]
    span = 8
    final = local_y // LANES - 1
    block = (1, span, local_x, LANES)
    shape = jax.ShapeDtypeStruct((local_x, LANES), F32)
    first_y, last_y = pl.pallas_call(
        functools.partial(edge_kernel, span),
        grid=(local_z // span,),
        in_specs=[
            pl.BlockSpec(block, lambda k: (0, k, 0, 0)),
            pl.BlockSpec(block, lambda k: (0, k, 0, final)),
            pl.BlockSpec(block, lambda k: (1, k, 0, final)),
        ],
        out_specs=[pl.BlockSpec((local_x, LANES), lambda k: (0, 0))] * 2,
        out_shape=[shape, shape],
        compiler_params=params(),
    )(opened, opened, wind)
    z_pair = shift_pair(opened[0, 0], wind[2, -1] * opened[0, -1], "gz")
    last_x = slice(local_x - 1, local_x)
    x_pair = shift_pair(opened[0, :, :1], wind[0, :, last_x] * opened[0, :, last_x], "gx")
    return z_pair + x_pair + shift_pair(first_y, last_y, "gy")


def divergence_kernel(wind, opened, over, z_low, z_high, x_low, x_high, y_low, y_high, out, face_z):
    step, steps = pl.program_id(0), pl.num_programs(0)
    span, local_x, local_y = out.shape
    lane = lax.broadcasted_iota(jnp.int32, (1, LANES), 1)
    for j in range(span):
        k = step * span + j
        before = None
        for i in range(local_x // 8):
            rows = slice(8 * i, 8 * i + 8)
            cells = opened[0, j, rows, :]
            if i < local_x // 8 - 1:
                after = opened[0, j, 8 * i + 8 : 8 * i + 16, :]
            else:
                after = jnp.broadcast_to(x_high[j], cells.shape)
            if before is None:
                before = jnp.broadcast_to(x_low[j] * cells[0:1], cells.shape)
            flux_x = wind[0, j, rows, :] * (cells * next_x(cells, after))
            right = pltpu.roll(y_high[rows, :], lax.rem(2 * LANES - 1 - k, LANES), 1)
            left = pltpu.roll(y_low[rows, :], lax.rem(LANES - k, LANES), 1)
            beside = next_y(cells)
            cut = local_y - LANES
            tail = jnp.where(lane == LANES - 1, right, beside[:, cut:])
            beside = tail if cut == 0 else jnp.concatenate([beside[:, :cut], tail], 1)
            flux_y = wind[1, j, rows, :] * (cells * beside)
            back = prev_y(flux_y)
            head = jnp.where(lane == 0, left * cells[:, :LANES], back[:, :LANES])
            back = head if cut == 0 else jnp.concatenate([head, back[:, LANES:]], 1)
            if j < span - 1:
                above = opened[0, j + 1, rows, :]
            else:
                above = jnp.where(step == steps - 1, z_high[rows, :], over[0, 0, rows, :])
            flux_z = wind[2, j, rows, :] * (cells * above)
            below = face_z[rows, :]
            if j == 0:
                below = jnp.where(step == 0, z_low[rows, :] * cells, below)
            out[j, rows, :] = (flux_x - prev_x(flux_x, before)) + (flux_y - back) + (flux_z - below)
            face_z[rows, :] = flux_z
            before = flux_x


def divergence(wind, opened, edges):
    local_z, local_x, local_y = wind.shape[1:]
    plane = pl.BlockSpec((local_x, local_y), lambda k: (0, 0))
    span = 4
    line = pl.BlockSpec((span, 1, local_y), lambda k: (k, 0, 0))
    pack = pl.BlockSpec((local_x, LANES), lambda k: (0, 0))
    return pl.pallas_call(
        divergence_kernel,
        grid=(local_z // span,),
        in_specs=[
            pl.BlockSpec((3, span, local_x, local_y), lambda k: (0, k, 0, 0)),
            pl.BlockSpec((1, span, local_x, local_y), lambda k: (0, k, 0, 0)),
            pl.BlockSpec(
                (1, 1, local_x, local_y),
                lambda k: (0, jnp.minimum(k * span + span, local_z - 1), 0, 0),
            ),
            plane,
            plane,
            line,
            line,
            pack,
            pack,
        ],
        out_specs=pl.BlockSpec((span, local_x, local_y), lambda k: (k, 0, 0)),
        out_shape=jax.ShapeDtypeStruct((local_z, local_x, local_y), F32),
        scratch_shapes=[pltpu.VMEM((local_x, local_y), F32)],
        compiler_params=params(),
    )(wind, opened, opened, *edges)


def limiter(demand, supply):
    binding = demand > supply
    return jnp.where(binding, supply / jnp.where(binding, demand, 1.0), 1.0)


def transport_kernel(local_z, scalar_count, *refs):
    scal, sc_halo = refs[0], refs[1:7]
    wind, opened, wi_halo = refs[7], refs[8], refs[9:15]
    mult, mu_halo = refs[15], refs[16:22]
    factor, wind_out, out = refs[22:25]
    speed, cell, kept = refs[25], refs[26], refs[27:]
    conc, trial, upper, lower, anti, ratio, low_z, lim_z, edge, result = (
        kept[at * scalar_count : (at + 1) * scalar_count] for at in range(10)
    )
    k = pl.program_id(0)
    local_x, local_y = out.shape[2:]
    lanes = local_y + LANES
    count = local_x // 8 + 2
    s1, s2, s3 = (lax.rem(k + 3 - d, 3) for d in range(1, 4))
    now, old = lax.rem(k, 2), lax.rem(k + 1, 2)

    def put_scalar(field, rows, wide, value):
        conc[field][now, rows, wide] = value

    def put_wind(field, rows, wide, value):
        cell[now, field, rows, wide] = value

    def put_mult(field, rows, wide, value):
        cell[now, 4, rows, wide] = value

    assemble(k, local_z, (scal,), sc_halo, put_scalar)
    assemble(k, local_z, (wind, opened), wi_halo, put_wind)
    assemble(k, local_z, (mult,), mu_halo, put_mult)

    def chunk(i):
        return pl.ds(pl.multiple_of(i * 8, 8), 8)

    def keep_ratios(s, mid, up_new, down_new):
        ratio[s][now, 0, mid, :] = up_new
        ratio[s][now, 1, mid, :] = down_new

    def keep(s, here, antis, lows, t_new, u_new, l_new):
        low_z[s][here, :] = lows[2]
        edge[s][0] = lows[0]
        trial[s][s1, here, :] = t_new
        upper[s][s1, here, :] = u_new
        lower[s][s1, here, :] = l_new
        for d in range(3):
            anti[s][s1, d, here, :] = antis[d]

    def limit(a, up_here, down_here, up_next, down_next):
        share = jnp.where(
            a >= 0.0, jnp.minimum(up_next, down_here), jnp.minimum(up_here, down_next)
        )
        return share * a

    def column(stages, i, _):
        last, mid, here, after = (chunk(i + d) for d in range(4))

        cells, multiplier = cell[old, 3, here, :], cell[old, 4, here, :]
        neighbours = (
            (next_x(cells, cell[old, 3, after, :]), next_x(multiplier, cell[old, 4, after, :])),
            (next_y(cells), next_y(multiplier)),
            (cell[now, 3, here, :], cell[now, 4, here, :]),
        )
        speeds, halves, sizes = [], [], []
        for d in range(3):
            open_next, mult_next = neighbours[d]
            face = cells * open_next
            value = (cell[old, d, here, :] * face + GAINS[d] * (mult_next - multiplier)) * face
            speeds.append(value)
            halves.append((0.5 * TIME_STEP) * value)
            sizes.append(jnp.abs(halves[-1]))
        for d in range(3):
            speed[d, here, :] = speeds[d][:, :local_y]

        for s in range(scalar_count):
            c = conc[s][old, here, :]
            downwind = (next_x(c, conc[s][old, after, :]), next_y(c), conc[s][now, here, :])
            antis, lows = [], []
            for d in range(3):
                a = sizes[d] * (downwind[d] - c)
                antis.append(a)
                lows.append(halves[d] * (downwind[d] + c) - a)
            change = (lows[0] - prev_x(lows[0], edge[s][0])) + (lows[1] - prev_y(lows[1]))
            t_new = c - (change + (lows[2] - low_z[s][here, :]))
            u_new, l_new = jnp.maximum(c, t_new), jnp.minimum(c, t_new)

            new = (here, antis, lows, t_new, u_new, l_new)
            if stages == 1:
                keep(s, *new)
                continue

            u, l = upper[s][s2, mid, :], lower[s][s2, mid, :]
            ceiling = jnp.maximum(
                jnp.maximum(u, upper[s][s1, mid, :]),
                jnp.maximum(
                    next_x(u, upper[s][s2, here, :]), prev_x(u, upper[s][s2, last, :])
                ),
            )
            ceiling = jnp.maximum(
                jnp.maximum(ceiling, upper[s][s3, mid, :]), jnp.maximum(next_y(u), prev_y(u))
            )
            bottom = jnp.minimum(
                jnp.minimum(l, lower[s][s1, mid, :]),
                jnp.minimum(
                    next_x(l, lower[s][s2, here, :]), prev_x(l, lower[s][s2, last, :])
                ),
            )
            bottom = jnp.minimum(
                jnp.minimum(bottom, lower[s][s3, mid, :]), jnp.minimum(next_y(l), prev_y(l))
            )
            a_x, a_y, a_z = (anti[s][s2, d, mid, :] for d in range(3))
            befores = (
                prev_x(a_x, anti[s][s2, 0, last, :]),
                prev_y(a_y),
                anti[s][s3, 2, mid, :],
            )
            inflow, outflow = 0.0, 0.0
            for a, b in zip((a_x, a_y, a_z), befores):
                inflow = inflow + (jnp.maximum(b, 0.0) - jnp.minimum(a, 0.0))
                outflow = outflow + (jnp.maximum(a, 0.0) - jnp.minimum(b, 0.0))
            t_mid = trial[s][s2, mid, :]
            up_new = limiter(inflow, ceiling - t_mid)
            down_new = limiter(outflow, t_mid - bottom)

            ratios = (mid, up_new, down_new)
            if stages == 2:
                keep(s, *new)
                keep_ratios(s, *ratios)
                continue

            r_up, r_down = ratio[s][old, 0, last, :], ratio[s][old, 1, last, :]
            own_up, own_down = r_up[:, :local_y], r_down[:, :local_y]
            own = slice(0, local_y)
            limited = (
                limit(
                    anti[s][s3, 0, last, own],
                    own_up,
                    own_down,
                    next_x(own_up, ratio[s][old, 0, mid, own]),
                    next_x(own_down, ratio[s][old, 1, mid, own]),
                ),
                limit(anti[s][s3, 1, last, :], r_up, r_down, next_y(r_up), next_y(r_down)),
                limit(
                    anti[s][s3, 2, last, own],
                    own_up,
                    own_down,
                    ratio[s][now, 0, last, own],
                    ratio[s][now, 1, last, own],
                ),
            )
            moved = limited[0] - prev_x(limited[0], edge[s][1, :, own])
            moved = moved + (limited[1] - prev_y(limited[1]))[:, :local_y]
            moved = moved + (limited[2] - lim_z[s][last, :])
            result[s][last, :] = trial[s][s3, last, own] - moved
            lim_z[s][last, :] = limited[2]
            edge[s][1, :, own] = limited[0]
            keep_ratios(s, *ratios)
            keep(s, *new)
        return 0

    for stages, begin, end in ((1, 1, 4), (2, 4, 5), (3, 5, local_z + 2 * W)):

        @pl.when((k >= begin) & (k < end))
        def _():
            lax.fori_loop(0, count + 1, functools.partial(column, stages), 0)

    inner = slice(LEAD + RX, LEAD + RX + local_x)

    @pl.when((k > W) & (k <= W + local_z))
    def _():
        for d in range(3):
            wind_out[d, 0] = speed[d, inner, :]

    @pl.when(k > 2 * W)
    def _():
        for s in range(scalar_count):
            out[s, 0] = result[s][inner, :]

    @pl.when(k == 2 * W)
    def _():
        for s in range(scalar_count):
            out[s, 0] = result[s][inner, :] * factor[s]


def transport(scalars, sc_halo, wind, opened, wi_halo, mult, mu_halo, factor):
    n, local_z, local_x, local_y = scalars.shape
    same = lambda k: k
    middle = lambda k: (0, jnp.clip(k - W, 0, local_z - 1), 0, 0)
    lanes = local_y + LANES
    rows = local_x + 2 * RX + 2 * LEAD
    plane = (rows, lanes)

    def main(count):
        return [pl.BlockSpec((count, 1, local_x, local_y), middle)]

    def halo(count):
        return halo_specs(count, local_z, local_x, local_y, same)

    return pl.pallas_call(
        functools.partial(transport_kernel, local_z, n),
        grid=(local_z + 2 * W,),
        in_specs=main(n)
        + halo(n)
        + main(3)
        + main(1)
        + halo(4)
        + main(1)
        + halo(1)
        + [pl.BlockSpec((n, local_x, local_y), lambda k: (0, 0, 0))],
        out_specs=[
            pl.BlockSpec(
                (3, 1, local_x, local_y), lambda k: (0, jnp.clip(k - 1 - W, 0, local_z - 1), 0, 0)
            ),
            pl.BlockSpec(
                (n, 1, local_x, local_y), lambda k: (0, jnp.clip(k - 2 * W, 0, local_z - 1), 0, 0)
            ),
        ],
        out_shape=[
            jax.ShapeDtypeStruct((3, local_z, local_x, local_y), F32),
            jax.ShapeDtypeStruct(scalars.shape, F32),
        ],
        scratch_shapes=[pltpu.VMEM((3, rows, local_y), F32), pltpu.VMEM((2, 5) + plane, F32)]
        + [
            pltpu.VMEM(shape, F32)
            for shape in (
                (2,) + plane,
                (3,) + plane,
                (3,) + plane,
                (3,) + plane,
                (3, 3) + plane,
                (2, 2) + plane,
                plane,
                (rows, local_y),
                (2, 8, lanes),
                (rows, local_y),
            )
            for _ in range(n)
        ],
        compiler_params=params(),
    )(scalars, *sc_halo, wind, opened, *wi_halo, mult, *mu_halo, factor)


def ground_factor(surface_flags):
    rates = 1.0 - TIME_STEP * np.asarray(DEPOSIT, np.float32)
    factor = jnp.zeros((len(DEPOSIT),) + surface_flags.shape, F32)
    for surface in range(4):
        column = jnp.asarray(rates[:, surface], F32)[:, None, None]
        factor = factor + jnp.where(surface_flags[None] == surface, column, 0.0)
    return jnp.where(lax.axis_index("gz") == 0, factor, 1.0)


def body(initial_wind, building_mask, surface_flags, scalars):
    opened = (1.0 - building_mask.astype(F32))[None]
    edges = face_edges(initial_wind, opened)
    sets = [(initial_wind, opened), (scalars,)]
    sets_z = [z_halo(arrays, edges[:2]) for arrays in sets]
    source = divergence(initial_wind, opened, edges)
    multiplier, (wind_halo, scalar_halo) = solve(source, sets, sets_z)
    multiplier = multiplier[None]
    mult_halo = halos((multiplier,))
    corrected, transported = transport(
        scalars,
        scalar_halo,
        initial_wind,
        opened,
        wind_halo,
        multiplier,
        mult_halo,
        ground_factor(surface_flags),
    )
    return (corrected, transported)


def solution(mesh):
    in_specs = (
        P(None, "gz", "gx", "gy"),
        P("gz", "gx", "gy"),
        P("gx", "gy"),
        P(None, "gz", "gx", "gy"),
    )
    out_specs = (P(None, "gz", "gx", "gy"), P(None, "gz", "gx", "gy"))
    return jax.shard_map(body, mesh=mesh, in_specs=in_specs, out_specs=out_specs, check_vma=False)
```
